128 devices in a mesh: sec: 16 (over x, y), sub: 8 (over z, core).
Axes of the slice: x: 4, y: 4, z: 4, core: 2. Of those that a mesh axis runs over, the one named last changes fastest.
Arguments:
- charges: bfloat16 [32768, 128], P(('sec', 'sub')), may hold values from -6 to 6
- positions: float32 [3, 32768, 128], P(None, ('sec', 'sub')), may hold values from 0 to 1
- p2m: bfloat16 [128, 128], replicated, may hold values from -0.5 to 0.5
- m2m: bfloat16 [8, 128, 128], replicated, may hold values from -0.1875 to 0.1875
- m2l: bfloat16 [316, 128, 128], replicated, may hold values from -0.0390625 to 0.0390625
- l2l: bfloat16 [8, 128, 128], replicated, may hold values from -0.5 to 0.5
- l2p: bfloat16 [128, 128], replicated, may hold values from -0.5 to 0.5
- send_rows: int32 [128, 128, 32], P(('sec', 'sub')), may hold values from 0 to 255
- send_counts: int32 [128, 128], P(('sec', 'sub')), may hold values from 1 to 32, as said below
- leaf_list: int32 [32768, 189], P(('sec', 'sub')), may hold values from 0 to 4351, as said below
- leaf_types: int32 [32768, 189], P(('sec', 'sub')), may hold values from 0 to 315, as said below
- parent_list: int32 [4096, 189], P(('sec', 'sub')), may hold values from 0 to 4095
- parent_types: int32 [4096, 189], P(('sec', 'sub')), may hold values from 0 to 315, as said below
- near_list: int32 [16, 32768, 128], P(None, ('sec', 'sub')), may hold values from 0 to 1024
Outputs:
- potential: float32 [32768, 128], P(('sec', 'sub'))
The draws below stay inside these ranges and needn't reach their ends.
Inputs may be any that keep to these rules, and one draw needn't show every extreme that they name: `send_counts`: the live slots of every block are at least one; in every draw some owner receives full blocks of 32 from every source. `leaf_list`: every entry names a live slot of a received block or one of the owner's own leaves. `leaf_types`: the 189 entries of one row are distinct translation vectors. `parent_types`: the 189 entries of one row are distinct translation vectors.
All inputs are finite; a program needn't handle non-finite values.
Results may differ from the reference program's by a relative error of at most 0.006.
Values may be sent and summed in bfloat16 or wider, within the bound.
A program may use at most 128 MiB of HBM per device.

```python
import jax
import jax.numpy as jnp
from jax import lax

P_SIZE = 128
PAN = 128
NT = 316
K = 189
NB = 16
CAP = 32
RIM = 512
LEAF_DEV = 256
LEAVES = 32768
PARENTS = 4096
N_SEC = 16
N_SUB = 8


def count_table(key):
    devices = N_SEC * N_SUB
    key = jax.random.fold_in(key, 101)
    key_level, key_raw, key_full = jax.random.split(key, 3)
    level = jax.random.randint(key_level, (devices,), 1, 5)
    upper = jnp.maximum(CAP * level // 4, 1)
    raw = jax.random.randint(key_raw, (devices, devices), 0, 1 << 20)
    counts = 1 + raw % upper[None, :]
    chosen = jax.random.randint(key_full, (), 0, devices)
    full = jnp.arange(devices, dtype=jnp.int32)[None, :] == chosen
    return jnp.where(full, CAP, counts).astype(jnp.int32)


def distinct_kinds(key, count):
    scores = jax.random.randint(key, (count, NT), 0, 1 << 20) * NT + jnp.arange(NT, dtype=jnp.int32)[None, :]
    columns = jnp.arange(NT, dtype=jnp.int32)[None, :]
    first_row = (jnp.arange(count, dtype=jnp.int32) == 0)[:, None]
    ends = (columns == 0) | (columns == NT - 1)
    scores = jnp.where(first_row & ends, (1 << 21) * NT + columns, scores)
    values, picked = lax.top_k(scores, K)
    return picked.astype(jnp.int32)


def draw_send_counts(key, part):
    return count_table(key)


def draw_leaf_list(key, part):
    counts = count_table(key)
    key = jax.random.fold_in(key, 7)
    devices = N_SEC * N_SUB
    key_src, key_pick, key_local, key_far = jax.random.split(key, 4)
    owner = (jnp.arange(LEAVES, dtype=jnp.int32) // LEAF_DEV)[:, None]
    source = jax.random.randint(key_src, (LEAVES, K), 0, devices)
    picked = jax.random.randint(key_pick, (LEAVES, K), 0, 1 << 20) % counts[source, owner]
    remote = source * CAP + picked
    local = devices * CAP + jax.random.randint(key_local, (LEAVES, K), 0, LEAF_DEV)
    farther = jax.random.randint(key_far, (LEAVES, K), 0, 2) == 0
    entries = jnp.where(farther, remote, local)
    within = (jnp.arange(LEAVES, dtype=jnp.int32) % LEAF_DEV)[:, None]
    column = jnp.arange(K, dtype=jnp.int32)[None, :] == 0
    entries = jnp.where(column & (within == 0), devices * CAP + LEAF_DEV - 1, entries)
    entries = jnp.where(column & (within == 1), 0, entries)
    return entries.astype(jnp.int32)


def draw_leaf_types(key, part):
    key = jax.random.fold_in(key, 21)
    return distinct_kinds(key, LEAVES)


def draw_parent_types(key, part):
    key = jax.random.fold_in(key, 23)
    return distinct_kinds(key, PARENTS)


def draw_near_list(key, part):
    key = jax.random.fold_in(key, 11)
    offset = jax.random.randint(key, (NB, LEAVES, PAN), -RIM, RIM + 1)
    place = (jnp.arange(LEAVES, dtype=jnp.int32) % LEAF_DEV)[:, None] * PAN + jnp.arange(PAN, dtype=jnp.int32)[None, :]
    leading = (jnp.arange(NB, dtype=jnp.int32) == 0)[:, None, None]
    offset = jnp.where(leading & (place == 0)[None], -RIM, offset)
    offset = jnp.where(leading & (place == LEAF_DEV * PAN - 1)[None], RIM, offset)
    return (offset + RIM).astype(jnp.int32)


def touch_ends(values, own_key, low, high):
    extent = values.shape
    index_at = [jax.random.randint(jax.random.fold_in(own_key, axis), (), 0, extent[axis]) for axis in range(len(extent))]
    values = values.at[tuple(index_at)].set(low)
    longest = extent.index(max(extent))
    index_at[longest] = (index_at[longest] + 1) % extent[longest]
    return values.at[tuple(index_at)].set(high)


def block_levels(key, extent, cuts, least, high):
    level, own = 1.0, jax.random.fold_in(key, 6)
    for position, shards_of in cuts:
        steps = jnp.exp(jax.random.uniform(jax.random.fold_in(own, position), (shards_of,), jnp.float32, least / len(cuts), high / len(cuts)))
        level = level * jnp.repeat(steps, extent[position] // shards_of).reshape([-1 if axis == position else 1 for axis in range(len(extent))])
    return level


def centred(rng, extent, deviation, reach, pieces=(), kind=jnp.bfloat16):
    values = deviation * jax.random.normal(rng, extent, jnp.float32)
    if pieces:
        values = values * block_levels(rng, extent, pieces, -0.22, 0.18)
    return jnp.clip(values, -reach, reach).astype(kind)


def setup_inputs(seed: int = 0) -> dict:
    splits = jax.random.split(jax.random.key(seed), 15)
    charges = centred(splits[0], (LEAVES, PAN), 1.0, 6.0, ((0, 128),))
    positions = jnp.clip(1.0 * jax.random.uniform(splits[1], (3, LEAVES, PAN), jnp.float32) ** block_levels(splits[1], (3, LEAVES, PAN), ((1, 128),), -0.2, 0.2), 0.0, 1.0)
    p2m = centred(splits[2], (PAN, P_SIZE), PAN ** -0.5, 0.5)
    m2m = centred(splits[3], (8, P_SIZE, P_SIZE), (8 * P_SIZE) ** -0.5, 0.1875)
    m2l = centred(splits[4], (NT, P_SIZE, P_SIZE), (P_SIZE * K) ** -0.5, 0.0390625)
    l2l = centred(splits[5], (8, P_SIZE, P_SIZE), P_SIZE ** -0.5, 0.5)
    l2p = centred(splits[6], (P_SIZE, PAN), P_SIZE ** -0.5, 0.5)
    send_rows = touch_ends(jax.random.randint(splits[7], (N_SEC * N_SUB, N_SEC * N_SUB, CAP), 0, LEAF_DEV), jax.random.fold_in(splits[7], 1), 0, LEAF_DEV - 1).astype(jnp.int32)
    send_counts = draw_send_counts(jax.random.fold_in(splits[14], 71), 0)
    leaf_list = draw_leaf_list(jax.random.fold_in(splits[14], 71), 0)
    leaf_types = draw_leaf_types(jax.random.fold_in(splits[14], 71), 0)
    parent_list = touch_ends(jax.random.randint(splits[11], (PARENTS, K), 0, PARENTS), jax.random.fold_in(splits[11], 1), 0, PARENTS - 1).astype(jnp.int32)
    parent_types = draw_parent_types(jax.random.fold_in(splits[14], 71), 0)
    near_list = draw_near_list(jax.random.fold_in(splits[14], 71), 0)
    return {"charges": charges, "positions": positions, "p2m": p2m, "m2m": m2m, "m2l": m2l, "l2l": l2l, "l2p": l2p, "send_rows": send_rows, "send_counts": send_counts, "leaf_list": leaf_list, "leaf_types": leaf_types, "parent_list": parent_list, "parent_types": parent_types, "near_list": near_list}


softening = 0.0025

def apply_kinds(sources, kinds, m2l):
    kind_count = m2l.shape[0]
    onehot = (kinds[..., None] == jnp.arange(kind_count, dtype=jnp.int32)).astype(jnp.float32)
    grouped = jnp.einsum('bkt,bkp->btp', onehot, sources.astype(jnp.float32))
    return jnp.einsum('btp,tpq->bq', grouped, m2l.astype(jnp.float32))

def blockwise(table, lists, kinds, m2l):
    count = lists.shape[0]
    block = min(count, 128)
    lists_b = lists.reshape(count // block, block, lists.shape[1])
    kinds_b = kinds.reshape(count // block, block, kinds.shape[1])

    def one_block(pair):
        return apply_kinds(table[pair[0]], pair[1], m2l)
    return lax.map(one_block, (lists_b, kinds_b)).reshape(count, m2l.shape[2])

def reference(charges, positions, p2m, m2m, m2l, l2l, l2p, send_rows, send_counts, leaf_list, leaf_types, parent_list, parent_types, near_list):
    devices = N_SEC * N_SUB
    multipole = jnp.dot(charges, p2m, preferred_element_type=jnp.float32).astype(jnp.bfloat16)
    children = multipole.reshape(PARENTS, 8, P_SIZE).astype(jnp.float32)
    parent_multipole = jnp.einsum('cop,opq->cq', children, m2m.astype(jnp.float32)).astype(jnp.bfloat16)
    parent_local = blockwise(parent_multipole, parent_list, parent_types, m2l).astype(jnp.bfloat16)
    downward = jnp.einsum('cp,opq->coq', parent_local.astype(jnp.float32), l2l.astype(jnp.float32)).reshape(LEAVES, P_SIZE)

    def one_device(device):
        slot_rows = lax.dynamic_slice_in_dim(send_rows, device, 1, 1)[:, 0, :]
        live = lax.dynamic_slice_in_dim(send_counts, device, 1, 1)[:, 0]
        index = jnp.arange(devices, dtype=jnp.int32)[:, None] * LEAF_DEV + slot_rows
        keep = jnp.arange(CAP, dtype=jnp.int32)[None, :] < live[:, None]
        remote = jnp.where(keep[..., None], multipole[index], jnp.zeros((), jnp.bfloat16))
        start = (device * LEAF_DEV).astype(jnp.int32)
        own = lax.dynamic_slice_in_dim(multipole, start, LEAF_DEV, 0)
        table = jnp.concatenate([remote.reshape(devices * CAP, P_SIZE), own], 0)
        lists = lax.dynamic_slice_in_dim(leaf_list, start, LEAF_DEV, 0)
        kinds = lax.dynamic_slice_in_dim(leaf_types, start, LEAF_DEV, 0)
        return blockwise(table, lists, kinds, m2l)
    leaf_local = lax.map(one_device, jnp.arange(devices, dtype=jnp.int32)).reshape(LEAVES, P_SIZE)
    leaf_total = (leaf_local + downward).astype(jnp.bfloat16)
    far = jnp.dot(leaf_total, l2p, preferred_element_type=jnp.float32)
    strength = jnp.pad(charges.astype(jnp.float32).reshape(-1), (RIM, RIM))
    centres = jnp.pad(positions.reshape(3, LEAVES * PAN), ((0, 0), (RIM, RIM)))
    panel_index = (jnp.arange(LEAVES, dtype=jnp.int32)[:, None] * PAN + jnp.arange(PAN, dtype=jnp.int32)[None, :]).astype(jnp.int32)
    own_pos = positions

    def add_neighbour(step, total):
        target = panel_index + near_list[step]
        gap = jnp.zeros((LEAVES, PAN), jnp.float32)
        for axis_c in range(3):
            delta = own_pos[axis_c] - centres[axis_c][target]
            gap = gap + delta * delta
        return total + strength[target] / jnp.sqrt(gap + softening)
    near = lax.fori_loop(0, NB, add_neighbour, jnp.zeros((LEAVES, PAN), jnp.float32)) / NB
    return far + near
```

```python
import functools

import jax
import jax.numpy as jnp
from jax import lax
from jax.experimental import pallas as pl
from jax.experimental.pallas import tpu as pltpu
from jax.sharding import PartitionSpec as P

RIM = 512
SOFT = 0.0025
BOTH = ("sec", "sub")
F32 = jnp.float32
BF16 = jnp.bfloat16
I32 = jnp.int32
SMEM = pl.BlockSpec(memory_space=pltpu.SMEM)
VMEM = pl.BlockSpec(memory_space=pltpu.VMEM)
ANY = pl.BlockSpec(memory_space=pl.ANY)


def passed_along(block, axis, distance):
    devices = range(lax.axis_size(axis))
    route = [(i - distance, i) for i in devices if i - distance in devices]
    return lax.ppermute(block, axis, route)


def prepare_kernel(rows_ref, charges_ref, p2m_ref, m2m_ref, mult_ref, parent_ref, out_ref, wide, block):
    mult = jnp.dot(charges_ref[...], p2m_ref[...], preferred_element_type=F32).astype(BF16)
    mult_ref[...] = mult
    wide[...] = mult.astype(F32)
    parents = parent_ref.shape[0]
    total = jnp.zeros(parent_ref.shape, F32)
    for octant in range(8):
        child = wide[pl.ds(octant, parents, stride=8), :].astype(BF16)
        total = total + jnp.dot(child, m2m_ref[octant], preferred_element_type=F32)
    parent_ref[...] = total.astype(BF16)
    step = block.shape[0]

    def some(g, carry):
        rows = rows_ref.at[pl.ds(g * step, step)]
        for u in range(step):
            block[pl.ds(u, 1), :] = wide[pl.ds(rows[u], 1), :]
        out_ref[pl.ds(pl.multiple_of(g * step, step), step), :] = block[...].astype(BF16)
        return carry

    lax.fori_loop(0, out_ref.shape[0] // step, some, 0)


def prepare(rows, charges, p2m, m2m):
    leaf_dev, coeffs = charges.shape[0], p2m.shape[1]
    return pl.pallas_call(
        prepare_kernel,
        out_shape=(
            jax.ShapeDtypeStruct((leaf_dev, coeffs), BF16),
            jax.ShapeDtypeStruct((leaf_dev // 8, coeffs), BF16),
            jax.ShapeDtypeStruct((rows.shape[0], coeffs), BF16),
        ),
        in_specs=[SMEM, VMEM, VMEM, VMEM],
        out_specs=(VMEM, VMEM, VMEM),
        scratch_shapes=[pltpu.VMEM((leaf_dev, coeffs), F32), pltpu.VMEM((128, coeffs), F32)],
        compiler_params=pltpu.CompilerParams(vmem_limit_bytes=32 << 20),
        name="prepare",
    )(rows, charges, p2m, m2m)


Z_SCALE = 2.0**-10


def near_kernel(pos_ref, charge_ref, low_ref, high_ref, list_ref, near_ref, xy, zq):
    leaf_dev, panels = near_ref.shape
    rim = low_ref.shape[1]

    def store(x, y, z, q, first, count):
        whole_x = jnp.round(x * 65535.0).astype(I32) - 32768
        whole_y = jnp.round(y * 65535.0).astype(I32)
        xy[pl.ds(first, count), :] = whole_x * 65536 + whole_y
        zq[pl.ds(first, count), :] = q * (1.0 + (z - 0.5) * Z_SCALE)

    store(low_ref[0], low_ref[1], low_ref[2], low_ref[3], 0, rim)
    store(pos_ref[0], pos_ref[1], pos_ref[2], charge_ref[...].astype(F32), rim, leaf_dev)
    store(high_ref[0], high_ref[1], high_ref[2], high_ref[3], rim + leaf_dev, rim)
    lane = lax.broadcasted_iota(I32, (8, panels), 1)
    shifts = 2 * rim + 1

    def group(g, carry):
        base = pl.multiple_of(g * 8, 8)
        x = pos_ref[0, pl.ds(base, 8), :]
        y = pos_ref[1, pl.ds(base, 8), :]
        z = pos_ref[2, pl.ds(base, 8), :]
        total = jnp.zeros((8, panels), F32)
        for n in range(list_ref.shape[0]):
            target = list_ref[n, pl.ds(base, 8), :] + lane
            which = target >> 7
            place = target & (panels - 1)
            word = jnp.zeros((8, panels), I32)
            weight = jnp.zeros((8, panels), F32)
            for q in range(shifts):
                at = which == q
                word = jnp.where(at, jnp.take_along_axis(xy[pl.ds(base + q, 8), :], place, axis=1), word)
                weight = jnp.where(at, jnp.take_along_axis(zq[pl.ds(base + q, 8), :], place, axis=1), weight)
            strength = weight.astype(BF16).astype(F32)
            safe = jnp.where(strength == 0.0, 1.0, strength)
            far_z = (weight - strength) / safe * (1.0 / Z_SCALE) + 0.5
            far_x = ((word >> 16) + 32768).astype(F32) * (1.0 / 65535.0)
            far_y = (word & 65535).astype(F32) * (1.0 / 65535.0)
            dx, dy, dz = x - far_x, y - far_y, z - far_z
            total = total + strength * lax.rsqrt(dx * dx + dy * dy + dz * dz + SOFT)
        near_ref[pl.ds(base, 8), :] = total * (1.0 / list_ref.shape[0])
        return carry

    lax.fori_loop(0, leaf_dev // 8, group, 0)


def near_field(positions, charges, low, high, near_list):
    leaf_dev, panels = charges.shape
    full = leaf_dev + 2 * low.shape[1]
    return pl.pallas_call(
        near_kernel,
        out_shape=jax.ShapeDtypeStruct((leaf_dev, panels), F32),
        in_specs=[VMEM] * 5,
        out_specs=VMEM,
        scratch_shapes=[pltpu.VMEM((full, panels), I32), pltpu.VMEM((full, panels), F32)],
        compiler_params=pltpu.CompilerParams(vmem_limit_bytes=32 << 20),
        cost_estimate=pl.CostEstimate(flops=30_000_000_00, bytes_accessed=4_000_000, transcendentals=1_000_000),
        name="near",
    )(positions, charges, low, high, near_list)


GROUP = 16
HALF = 8


def far_kernel(
    lists_hbm, types_ref, arrived_ref, own_ref, parents_ref, m2l_hbm, l2l_ref, l2p_ref, near_ref, out_ref,
    table, rows, tall, grouped, m2l, total, index_a, index_b, sems,
):
    boxes = types_ref.shape[0]
    wide = types_ref.shape[1]
    kinds, coeffs = m2l.shape[0], m2l.shape[2]
    steps = boxes // GROUP
    entries = index_a.shape[1]
    rows[...] = jnp.zeros_like(rows)

    def fetch(block, buffer, which):
        at = pl.multiple_of(block * HALF, HALF)
        return pltpu.make_async_copy(lists_hbm.at[pl.ds(at, HALF), :], buffer, sems.at[which])

    weights = pltpu.make_async_copy(m2l_hbm, m2l, sems.at[2])
    fetch(0, index_a, 0).start()
    fetch(1, index_b, 1).start()
    weights.start()
    first = 0
    for source in (arrived_ref, own_ref, parents_ref):
        count = source.shape[0]
        table[pl.ds(first, count), :] = source[...].astype(F32)
        first += count
    kind_of = lax.broadcasted_iota(I32, (tall.shape[0] // GROUP, wide), 0)

    def some(step, carry):
        for half, index in ((0, index_a), (1, index_b)):
            fetch(step * 2 + half, index, half).wait()
            for j in range(HALF):
                box = half * HALF + j
                for k in range(entries):
                    rows[pl.ds(box * wide + k, 1), :] = table[pl.ds(index[j, k], 1), :]

            @pl.when(step + 1 < steps)
            def _():
                fetch((step + 1) * 2 + half, index, half).start()

            for j in range(HALF):
                box = half * HALF + j
                kind = types_ref[pl.ds(step * GROUP + box, 1), :]
                onehot = (kind_of == kind).astype(BF16)
                picked = rows[pl.ds(box * wide, wide), :].astype(BF16)
                tall[pl.ds(box, kind_of.shape[0], stride=GROUP), :] = jnp.dot(onehot, picked, preferred_element_type=F32)
        at = pl.multiple_of(step * GROUP, GROUP)
        for t in range(kinds):
            grouped[t, pl.ds(at, GROUP), :] = tall[pl.ds(t * GROUP, GROUP), :].astype(BF16)
        return carry

    lax.fori_loop(0, steps, some, 0)
    weights.wait()
    total[...] = jnp.zeros_like(total)
    chunk = 12

    def multiply(first, count):
        left = jnp.concatenate([grouped[first + t] for t in range(count)], axis=1)
        right = m2l[pl.ds(first, count)].reshape(count * coeffs, coeffs)
        total[...] += jnp.dot(left, right, preferred_element_type=F32)

    def several(i, carry):
        multiply(i * chunk, chunk)
        return carry

    lax.fori_loop(0, kinds // chunk, several, 0)
    if kinds % chunk:
        multiply(kinds // chunk * chunk, kinds % chunk)
    leaf_dev = out_ref.shape[0]
    parents = boxes - leaf_dev
    parent_local = total[pl.ds(leaf_dev, parents), :].astype(BF16)
    for octant in range(8):
        down = jnp.dot(parent_local, l2l_ref[octant], preferred_element_type=F32)
        total[pl.ds(octant, parents, stride=8), :] += down
    leaf_total = total[pl.ds(0, leaf_dev), :].astype(BF16)
    out_ref[...] = jnp.dot(leaf_total, l2p_ref[...], preferred_element_type=F32) + near_ref[...]


def far_field(lists, types, arrived, own, parents, m2l, l2l, l2p, near):
    boxes, wide = types.shape
    kinds, coeffs = m2l.shape[0], m2l.shape[2]
    tables = arrived.shape[0] + own.shape[0] + parents.shape[0]
    kinds_up = -(-kinds // 16) * 16
    return pl.pallas_call(
        far_kernel,
        out_shape=jax.ShapeDtypeStruct(near.shape, F32),
        in_specs=[ANY, VMEM, VMEM, VMEM, VMEM, ANY, VMEM, VMEM, VMEM],
        out_specs=VMEM,
        scratch_shapes=[
            pltpu.VMEM((tables, coeffs), F32),
            pltpu.VMEM((GROUP * wide, coeffs), F32),
            pltpu.VMEM((kinds_up * GROUP, coeffs), F32),
            pltpu.VMEM((kinds, boxes, coeffs), BF16),
            pltpu.VMEM(m2l.shape, BF16),
            pltpu.VMEM((boxes, coeffs), F32),
            pltpu.SMEM((HALF, lists.shape[1]), I32),
            pltpu.SMEM((HALF, lists.shape[1]), I32),
            pltpu.SemaphoreType.DMA((3,)),
        ],
        compiler_params=pltpu.CompilerParams(vmem_limit_bytes=56 << 20),
        name="far",
    )(lists, types, arrived, own, parents, m2l, l2l, l2p, near)


def local(
    charges, positions, p2m, m2m, m2l, l2l, l2p,
    send_rows, send_counts, leaf_list, leaf_types, parent_list, parent_types, near_list,
):
    leaf_dev, panels = charges.shape
    coeffs = p2m.shape[1]
    capacity = send_rows.shape[2]
    devices = lax.axis_size(BOTH)
    rim = RIM // panels
    edge = lambda part: jnp.concatenate([positions[:, part], charges[part].astype(F32)[None]], 0)
    low = passed_along(edge(slice(leaf_dev - rim, leaf_dev)), BOTH, 1)
    high = passed_along(edge(slice(0, rim)), BOTH, -1)
    own, parent_own, outgoing = prepare(send_rows.reshape(devices * capacity), charges, p2m, m2m)
    arrived = lax.all_to_all(
        outgoing.reshape(devices, capacity, coeffs), BOTH, split_axis=0, concat_axis=0, tiled=True
    ).reshape(devices * capacity, coeffs)
    parents = lax.all_gather(lax.all_gather(parent_own, "sub", axis=0, tiled=True), "sec", axis=0, tiled=True)
    near = near_field(positions, charges, low, high, near_list)
    entries = leaf_list.shape[1]
    wide = -(-entries // 16) * 16
    pad = ((0, 0), (0, wide - entries))
    lists = jnp.concatenate([leaf_list, parent_list + (devices * capacity + leaf_dev)], 0)
    types = jnp.concatenate([leaf_types, parent_types], 0)
    types = jnp.pad(types, pad, constant_values=-1)
    return far_field(lists, types, arrived, own, parents, m2l, l2l, l2p, near)


def solution(mesh):
    along = P(BOTH, None)
    in_specs = (
        along, P(None, BOTH, None), P(), P(), P(), P(), P(),
        P(BOTH, None, None), along, along, along, along, along, P(None, BOTH, None),
    )
    return jax.shard_map(local, mesh=mesh, in_specs=in_specs, out_specs=along, check_vma=False)
```

```python
import functools

import jax
import jax.numpy as jnp
from jax import lax
from jax.experimental import pallas as pl
from jax.experimental.pallas import tpu as pltpu
from jax.sharding import PartitionSpec as P

RIM = 512
SOFT = 0.0025
BOTH = ("sec", "sub")
F32 = jnp.float32
BF16 = jnp.bfloat16
I32 = jnp.int32
SMEM = pl.BlockSpec(memory_space=pltpu.SMEM)
VMEM = pl.BlockSpec(memory_space=pltpu.VMEM)
ANY = pl.BlockSpec(memory_space=pl.ANY)


def prepare_kernel(rows_ref, charges_ref, p2m_ref, m2m_ref, mult_ref, parent_ref, out_ref, wide, block):
    mult = jnp.dot(charges_ref[...], p2m_ref[...], preferred_element_type=F32).astype(BF16)
    mult_ref[...] = mult
    wide[...] = mult.astype(F32)
    parents = parent_ref.shape[0]
    total = jnp.zeros(parent_ref.shape, F32)
    for octant in range(8):
        child = wide[pl.ds(octant, parents, stride=8), :].astype(BF16)
        total = total + jnp.dot(child, m2m_ref[octant], preferred_element_type=F32)
    parent_ref[...] = total.astype(BF16)
    step = block.shape[0]

    def some(g, carry):
        rows = rows_ref.at[pl.ds(g * step, step)]
        for u in range(step):
            block[pl.ds(u, 1), :] = wide[pl.ds(rows[u], 1), :]
        out_ref[pl.ds(pl.multiple_of(g * step, step), step), :] = block[...].astype(BF16)
        return carry

    lax.fori_loop(0, out_ref.shape[0] // step, some, 0)


def prepare(rows, charges, p2m, m2m):
    leaf_dev, coeffs = charges.shape[0], p2m.shape[1]
    return pl.pallas_call(
        prepare_kernel,
        out_shape=(
            jax.ShapeDtypeStruct((leaf_dev, coeffs), BF16),
            jax.ShapeDtypeStruct((leaf_dev // 8, coeffs), BF16),
            jax.ShapeDtypeStruct((rows.shape[0], coeffs), BF16),
        ),
        in_specs=[SMEM, VMEM, VMEM, VMEM],
        out_specs=(VMEM, VMEM, VMEM),
        scratch_shapes=[pltpu.VMEM((leaf_dev, coeffs), F32), pltpu.VMEM((128, coeffs), F32)],
        compiler_params=pltpu.CompilerParams(vmem_limit_bytes=32 << 20),
        name="prepare",
    )(rows, charges, p2m, m2m)


Z_SCALE = 2.0**-10
EDGE = 8
MESH = pl.DeviceIdType.MESH


def exchange_kernel(
    n_sec, n_sub, out_ref, parent_ref, pos_ref, charge_ref, list_ref, arrived_ref, parents_ref, near_ref,
    edge, halo, xy, zq, send_sems, recv_sems, own_sems,
):
    devices = n_sec * n_sub
    me = lax.axis_index("sec") * n_sub + lax.axis_index("sub")
    cap = out_ref.shape[0] // devices
    share = parent_ref.shape[0]
    leaf_dev, panels = near_ref.shape

    def place_of(device):
        return (device // n_sub, device % n_sub)

    def other(distance):
        return (me + distance) % devices

    barrier = pltpu.get_barrier_semaphore()

    def greet(d, carry):
        pl.semaphore_signal(barrier, inc=1, device_id=place_of(other(d)), device_id_type=MESH)
        return carry

    lax.fori_loop(1, devices, greet, 0)
    for side, rows in ((0, pl.ds(leaf_dev - EDGE, EDGE)), (1, pl.ds(0, EDGE))):
        for axis in range(3):
            edge[side, axis] = pos_ref[axis, rows, :]
    charges = charge_ref[...].astype(F32)
    edge[0, 3] = charges[leaf_dev - EDGE :]
    edge[1, 3] = charges[:EDGE]
    pl.semaphore_wait(barrier, devices - 1)

    def to_side(side):
        return pltpu.make_async_remote_copy(
            src_ref=edge.at[side], dst_ref=halo.at[side], send_sem=send_sems.at[side], recv_sem=recv_sems.at[side],
            device_id=place_of(other(1 if side == 0 else devices - 1)), device_id_type=MESH,
        )

    def send(source, target, which, device):
        return pltpu.make_async_remote_copy(
            src_ref=source, dst_ref=target, send_sem=send_sems.at[which], recv_sem=recv_sems.at[which],
            device_id=place_of(device), device_id_type=MESH,
        )

    to_side(0).start()
    to_side(1).start()
    mine = pl.ds(pl.multiple_of(me * cap, cap), cap)
    mine_up = pl.ds(pl.multiple_of(me * share, share), share)

    def give(d, carry):
        device = other(d)
        send(out_ref.at[pl.ds(pl.multiple_of(device * cap, cap), cap), :], arrived_ref.at[mine, :], 2, device).start()
        send(parent_ref, parents_ref.at[mine_up, :], 3, device).start()
        return carry

    lax.fori_loop(1, devices, give, 0)
    own = pltpu.make_async_copy(out_ref.at[mine, :], arrived_ref.at[mine, :], own_sems.at[0])
    own_up = pltpu.make_async_copy(parent_ref, parents_ref.at[mine_up, :], own_sems.at[1])
    own.start()
    own_up.start()

    def store(x, y, z, q, first, count):
        whole_x = jnp.round(x * 65535.0).astype(I32) - 32768
        whole_y = jnp.round(y * 65535.0).astype(I32)
        xy[pl.ds(first, count), :] = whole_x * 65536 + whole_y
        zq[pl.ds(first, count), :] = q * (1.0 + (z - 0.5) * Z_SCALE)

    store(pos_ref[0], pos_ref[1], pos_ref[2], charges, EDGE, leaf_dev)
    for side, end, first in ((0, 0, 0), (1, devices - 1, EDGE + leaf_dev)):
        to_side(side).wait()
        strength = halo[side, 3] * jnp.where(me == end, 0.0, 1.0)
        store(halo[side, 0], halo[side, 1], halo[side, 2], strength, first, EDGE)
    lane = lax.broadcasted_iota(I32, (8, panels), 1)
    rim = RIM // panels

    def group(g, carry):
        base = pl.multiple_of(g * 8, 8)
        x = pos_ref[0, pl.ds(base, 8), :]
        y = pos_ref[1, pl.ds(base, 8), :]
        z = pos_ref[2, pl.ds(base, 8), :]
        total = jnp.zeros((8, panels), F32)
        for n in range(list_ref.shape[0]):
            target = list_ref[n, pl.ds(base, 8), :] + lane
            which = target >> 7
            place = target & (panels - 1)
            word = jnp.zeros((8, panels), I32)
            weight = jnp.zeros((8, panels), F32)
            for q in range(2 * rim + 1):
                at = which == q
                rows = pl.ds(base + (EDGE - rim + q), 8)
                word = jnp.where(at, jnp.take_along_axis(xy[rows, :], place, axis=1), word)
                weight = jnp.where(at, jnp.take_along_axis(zq[rows, :], place, axis=1), weight)
            strength = weight.astype(BF16).astype(F32)
            safe = jnp.where(strength == 0.0, 1.0, strength)
            far_z = (weight - strength) / safe * (1.0 / Z_SCALE) + 0.5
            far_x = ((word >> 16) + 32768).astype(F32) * (1.0 / 65535.0)
            far_y = (word & 65535).astype(F32) * (1.0 / 65535.0)
            dx, dy, dz = x - far_x, y - far_y, z - far_z
            total = total + strength * lax.rsqrt(dx * dx + dy * dy + dz * dz + SOFT)
        near_ref[pl.ds(base, 8), :] = total * (1.0 / list_ref.shape[0])
        return carry

    lax.fori_loop(0, leaf_dev // 8, group, 0)
    own.wait()
    own_up.wait()
    rest = pl.ds(0, (devices - 1) * cap)
    rest_up = pl.ds(0, (devices - 1) * share)
    all_leaves = send(out_ref.at[rest, :], arrived_ref.at[rest, :], 2, other(1))
    all_leaves.wait_recv()
    all_leaves.wait_send()
    all_parents = send(parents_ref.at[rest_up, :], parents_ref.at[rest_up, :], 3, other(1))
    all_parents.wait_recv()
    all_parents.wait_send()


def exchange(n_sec, n_sub, outgoing, parent_own, positions, charges, near_list):
    leaf_dev, panels = charges.shape
    coeffs = outgoing.shape[1]
    devices = n_sec * n_sub
    full = leaf_dev + 2 * EDGE
    return pl.pallas_call(
        functools.partial(exchange_kernel, n_sec, n_sub),
        out_shape=(
            jax.ShapeDtypeStruct(outgoing.shape, BF16),
            jax.ShapeDtypeStruct((devices * parent_own.shape[0], coeffs), BF16),
            jax.ShapeDtypeStruct((leaf_dev, panels), F32),
        ),
        in_specs=[VMEM] * 5,
        out_specs=(VMEM, VMEM, VMEM),
        scratch_shapes=[
            pltpu.VMEM((2, 4, EDGE, panels), F32),
            pltpu.VMEM((2, 4, EDGE, panels), F32),
            pltpu.VMEM((full, panels), I32),
            pltpu.VMEM((full, panels), F32),
            pltpu.SemaphoreType.DMA((4,)),
            pltpu.SemaphoreType.DMA((4,)),
            pltpu.SemaphoreType.DMA((2,)),
        ],
        compiler_params=pltpu.CompilerParams(vmem_limit_bytes=32 << 20, collective_id=0, has_side_effects=True),
        name="exchange",
    )(outgoing, parent_own, positions, charges, near_list)


GROUP = 16
QUAD = 4


def far_kernel(
    leaf_list_ref, parent_list_ref, leaf_types_ref, parent_types_ref, arrived_ref, own_ref, parents_ref,
    m2l_hbm, l2l_ref, l2p_ref, near_ref, out_ref,
    table, lists, types, rows, tall_a, tall_b, grouped, m2l, total, index_a, index_b, sems,
):
    leaf_dev = leaf_list_ref.shape[0]
    boxes, entries = lists.shape
    wide = rows.shape[0] // GROUP
    kinds, coeffs = m2l.shape[0], m2l.shape[2]
    steps = boxes // GROUP
    weights = pltpu.make_async_copy(m2l_hbm, m2l, sems.at[2])
    weights.start()
    leaf_rows = arrived_ref.shape[0] + own_ref.shape[0]
    lists[pl.ds(0, leaf_dev), :] = leaf_list_ref[...]
    lists[pl.ds(leaf_dev, boxes - leaf_dev), :] = parent_list_ref[...] + leaf_rows

    def fetch(step, buffer, which):
        at = pl.multiple_of(step * GROUP, GROUP)
        return pltpu.make_async_copy(lists.at[pl.ds(at, GROUP), :], buffer, sems.at[which])

    fetch(0, index_a, 0).start()
    fetch(1, index_b, 1).start()
    types[...] = jnp.full_like(types, -1)
    types[pl.ds(0, leaf_dev), pl.ds(0, entries)] = leaf_types_ref[...]
    types[pl.ds(leaf_dev, boxes - leaf_dev), pl.ds(0, entries)] = parent_types_ref[...]
    rows[...] = jnp.zeros_like(rows)
    tall_b[...] = jnp.zeros_like(tall_b)
    first = 0
    for source in (arrived_ref, own_ref, parents_ref):
        count = source.shape[0]
        table[pl.ds(first, count), :] = source[...].astype(F32)
        first += count
    kinds_up = tall_a.shape[1] // QUAD - 4
    kind_of = lax.broadcasted_iota(I32, (kinds_up, types.shape[1]), 0)
    upper = lax.broadcasted_iota(I32, (8, coeffs), 0) >= QUAD

    def pick(index):
        for box in range(GROUP):
            for k in range(entries):
                rows[pl.ds(box * wide + k, 1), :] = table[pl.ds(index[box, k], 1), :]

    def spread(tall, step):
        for box in range(GROUP):
            kind = types[pl.ds(step * GROUP + box, 1), :]
            onehot = (kind_of == kind).astype(BF16)
            picked = rows[pl.ds(box * wide, wide), :].astype(BF16)
            tall[box // QUAD, pl.ds(8 + box % QUAD, kinds_up, stride=QUAD), :] = jnp.dot(
                onehot, picked, preferred_element_type=F32
            )

    def turn(tall, step):
        at = pl.multiple_of(step * GROUP, GROUP)
        for t in range(kinds):
            pair = [
                jnp.where(upper, tall[2 * h + 1, pl.ds(8 + t * QUAD - QUAD, 8), :], tall[2 * h, pl.ds(8 + t * QUAD, 8), :])
                for h in range(2)
            ]
            grouped[t, pl.ds(at, GROUP), :] = jnp.concatenate(pair, 0).astype(BF16)

    def some(i, carry):
        for half, index, tall, done in ((0, index_a, tall_a, tall_b), (1, index_b, tall_b, tall_a)):
            step = i * 2 + half
            fetch(step, index, half).wait()
            pick(index)
            spread(tall, step)
            turn(done, jnp.maximum(step - 1, 0))
            fetch(jnp.minimum(step + 2, steps - 2 + half), index, half).start()
        return carry

    lax.fori_loop(0, steps // 2, some, 0)
    for half, index in ((0, index_a), (1, index_b)):
        fetch(steps - 2 + half, index, half).wait()
    turn(tall_b, steps - 1)
    weights.wait()
    total[...] = jnp.zeros_like(total)
    chunk = 12

    def multiply(first, count):
        left = jnp.concatenate([grouped[first + t] for t in range(count)], axis=1)
        right = m2l[pl.ds(first, count)].reshape(count * coeffs, coeffs)
        total[...] += jnp.dot(left, right, preferred_element_type=F32)

    def several(i, carry):
        multiply(i * chunk, chunk)
        return carry

    lax.fori_loop(0, kinds // chunk, several, 0)
    if kinds % chunk:
        multiply(kinds // chunk * chunk, kinds % chunk)
    parents = boxes - leaf_dev
    parent_local = total[pl.ds(leaf_dev, parents), :].astype(BF16)
    for octant in range(8):
        down = jnp.dot(parent_local, l2l_ref[octant], preferred_element_type=F32)
        total[pl.ds(octant, parents, stride=8), :] += down
    leaf_total = total[pl.ds(0, leaf_dev), :].astype(BF16)
    out_ref[...] = jnp.dot(leaf_total, l2p_ref[...], preferred_element_type=F32) + near_ref[...]


def far_field(leaf_list, parent_list, leaf_types, parent_types, arrived, own, parents, m2l, l2l, l2p, near):
    boxes, entries = leaf_list.shape[0] + parent_list.shape[0], leaf_list.shape[1]
    kinds, coeffs = m2l.shape[0], m2l.shape[2]
    tables = arrived.shape[0] + own.shape[0] + parents.shape[0]
    wide = -(-entries // 16) * 16
    kinds_up = -(-kinds // 16) * 16
    return pl.pallas_call(
        far_kernel,
        out_shape=jax.ShapeDtypeStruct(near.shape, F32),
        in_specs=[VMEM] * 7 + [ANY] + [VMEM] * 3,
        out_specs=VMEM,
        scratch_shapes=[
            pltpu.VMEM((tables, coeffs), F32),
            pltpu.VMEM((boxes, entries), I32),
            pltpu.VMEM((boxes, wide), I32),
            pltpu.VMEM((GROUP * wide, coeffs), F32),
            pltpu.VMEM((GROUP // QUAD, kinds_up * QUAD + 4 * QUAD, coeffs), F32),
            pltpu.VMEM((GROUP // QUAD, kinds_up * QUAD + 4 * QUAD, coeffs), F32),
            pltpu.VMEM((kinds, boxes, coeffs), BF16),
            pltpu.VMEM(m2l.shape, BF16),
            pltpu.VMEM((boxes, coeffs), F32),
            pltpu.SMEM((GROUP, entries), I32),
            pltpu.SMEM((GROUP, entries), I32),
            pltpu.SemaphoreType.DMA((3,)),
        ],
        compiler_params=pltpu.CompilerParams(vmem_limit_bytes=58 << 20),
        name="far",
    )(leaf_list, parent_list, leaf_types, parent_types, arrived, own, parents, m2l, l2l, l2p, near)


def local(
    charges, positions, p2m, m2m, m2l, l2l, l2p,
    send_rows, send_counts, leaf_list, leaf_types, parent_list, parent_types, near_list,
):
    n_sec, n_sub = lax.axis_size("sec"), lax.axis_size("sub")
    own, parent_own, outgoing = prepare(send_rows.reshape(n_sec * n_sub * send_rows.shape[2]), charges, p2m, m2m)
    arrived, parents, near = exchange(n_sec, n_sub, outgoing, parent_own, positions, charges, near_list)
    return far_field(leaf_list, parent_list, leaf_types, parent_types, arrived, own, parents, m2l, l2l, l2p, near)


def solution(mesh):
    along = P(BOTH, None)
    in_specs = (
        along, P(None, BOTH, None), P(), P(), P(), P(), P(),
        P(BOTH, None, None), along, along, along, along, along, P(None, BOTH, None),
    )
    return jax.shard_map(local, mesh=mesh, in_specs=in_specs, out_specs=along, check_vma=False)
```

```python
import functools

import jax
import jax.numpy as jnp
from jax import lax
from jax.experimental import pallas as pl
from jax.experimental.pallas import tpu as pltpu
from jax.sharding import PartitionSpec as P

RIM = 512
SOFT = 0.0025
BOTH = ("sec", "sub")
F32 = jnp.float32
BF16 = jnp.bfloat16
I32 = jnp.int32
SMEM = pl.BlockSpec(memory_space=pltpu.SMEM)
VMEM = pl.BlockSpec(memory_space=pltpu.VMEM)
ANY = pl.BlockSpec(memory_space=pl.ANY)


Z_SCALE = 2.0**-10
EDGE = 8
STRIDE = 37
MESH = pl.DeviceIdType.MESH


def exchange_kernel(
    n_sec, n_sub, rows_ref, charge_hbm, p2m_hbm, m2m_hbm, pos_hbm, list_hbm, own_ref, arrived_ref, parents_ref, near_ref,
    charge_ref, p2m_ref, m2m_ref, pos_ref, list_ref, wide, block, out_ref, parent_ref,
    edge, halo, xy, zq, in_sems, send_sems, recv_sems, own_sems,
):
    devices = n_sec * n_sub
    me = lax.axis_index("sec") * n_sub + lax.axis_index("sub")
    chip, core = me // 2, me % 2
    chips = devices // 2
    cap = out_ref.shape[0] // devices
    leaf_dev, panels = near_ref.shape

    def place_of(device):
        return (device // n_sub, device % n_sub)

    def other(distance):
        return (me + distance) % devices

    loads = [
        pltpu.make_async_copy(source, target, in_sems.at[i])
        for i, (source, target) in enumerate(
            ((charge_hbm, charge_ref), (p2m_hbm, p2m_ref), (m2m_hbm, m2m_ref), (pos_hbm, pos_ref), (list_hbm, list_ref))
        )
    ]
    for load in loads:
        load.start()
    barrier = pltpu.get_barrier_semaphore()

    def greet(d, carry):
        pl.semaphore_signal(barrier, inc=1, device_id=place_of(other((d * STRIDE) % devices)), device_id_type=MESH)
        return carry

    lax.fori_loop(1, devices, greet, 0)
    for load in loads[:3]:
        load.wait()
    mult = jnp.dot(charge_ref[...], p2m_ref[...], preferred_element_type=F32).astype(BF16)
    own_ref[...] = mult
    wide[...] = mult.astype(F32)
    share = parent_ref.shape[0]
    total = jnp.zeros(parent_ref.shape, F32)
    for octant in range(8):
        child = wide[pl.ds(octant, share, stride=8), :].astype(BF16)
        total = total + jnp.dot(child, m2m_ref[octant], preferred_element_type=F32)
    parent_ref[...] = total.astype(BF16)
    step = block.shape[0]

    def some(g, carry):
        rows = rows_ref.at[pl.ds(g * step, step)]
        for u in range(step):
            block[pl.ds(u, 1), :] = wide[pl.ds(rows[u], 1), :]
        out_ref[pl.ds(pl.multiple_of(g * step, step), step), :] = block[...].astype(BF16)
        return carry

    lax.fori_loop(0, out_ref.shape[0] // step, some, 0)
    loads[3].wait()
    for side, rows in ((0, pl.ds(leaf_dev - EDGE, EDGE)), (1, pl.ds(0, EDGE))):
        for axis in range(3):
            edge[side, axis] = pos_ref[axis, rows, :]
    charges = charge_ref[...].astype(F32)
    edge[0, 3] = charges[leaf_dev - EDGE :]
    edge[1, 3] = charges[:EDGE]
    pl.semaphore_wait(barrier, devices - 1)

    def send(source, target, which, device):
        return pltpu.make_async_remote_copy(
            src_ref=source, dst_ref=target, send_sem=send_sems.at[which], recv_sem=recv_sems.at[which],
            device_id=place_of(device), device_id_type=MESH,
        )

    def to_side(side):
        return send(edge.at[side], halo.at[side], side, other(1 if side == 0 else devices - 1))

    to_side(0).start()
    to_side(1).start()
    mine = pl.ds(pl.multiple_of(me * cap, cap), cap)

    def give_up(d, carry):
        send(parent_ref, parents_ref.at[chip, core], 3, other((2 * d * STRIDE) % devices)).start()
        return carry

    def give(d, carry):
        device = other((d * STRIDE) % devices)
        send(out_ref.at[pl.ds(pl.multiple_of(device * cap, cap), cap), :], arrived_ref.at[mine, :], 2, device).start()
        return carry

    lax.fori_loop(1, chips, give_up, 0)
    lax.fori_loop(1, devices, give, 0)
    own = pltpu.make_async_copy(out_ref.at[mine, :], arrived_ref.at[mine, :], own_sems.at[0])
    own_up = pltpu.make_async_copy(parent_ref, parents_ref.at[chip, core], own_sems.at[1])
    own.start()
    own_up.start()
    loads[4].wait()

    def store(x, y, z, q, first, count):
        whole_x = jnp.round(x * 65535.0).astype(I32) - 32768
        whole_y = jnp.round(y * 65535.0).astype(I32)
        xy[pl.ds(first, count), :] = whole_x * 65536 + whole_y
        zq[pl.ds(first, count), :] = q * (1.0 + (z - 0.5) * Z_SCALE)

    store(pos_ref[0], pos_ref[1], pos_ref[2], charges, EDGE, leaf_dev)
    for side, end, first in ((0, 0, 0), (1, devices - 1, EDGE + leaf_dev)):
        to_side(side).wait()
        strength = halo[side, 3] * jnp.where(me == end, 0.0, 1.0)
        store(halo[side, 0], halo[side, 1], halo[side, 2], strength, first, EDGE)
    lane = lax.broadcasted_iota(I32, (8, panels), 1)
    rim = RIM // panels

    def group(g, carry):
        base = pl.multiple_of(g * 8, 8)
        x = pos_ref[0, pl.ds(base, 8), :]
        y = pos_ref[1, pl.ds(base, 8), :]
        z = pos_ref[2, pl.ds(base, 8), :]
        total = jnp.zeros((8, panels), F32)
        for n in range(list_ref.shape[0]):
            target = list_ref[n, pl.ds(base, 8), :] + lane
            which = target >> 7
            place = target & (panels - 1)
            word = jnp.zeros((8, panels), I32)
            weight = jnp.zeros((8, panels), F32)
            for q in range(2 * rim + 1):
                at = which == q
                rows = pl.ds(base + (EDGE - rim + q), 8)
                word = jnp.where(at, jnp.take_along_axis(xy[rows, :], place, axis=1), word)
                weight = jnp.where(at, jnp.take_along_axis(zq[rows, :], place, axis=1), weight)
            strength = weight.astype(BF16).astype(F32)
            safe = jnp.where(strength == 0.0, 1.0, strength)
            far_z = (weight - strength) / safe * (1.0 / Z_SCALE) + 0.5
            far_x = ((word >> 16) + 32768).astype(F32) * (1.0 / 65535.0)
            far_y = (word & 65535).astype(F32) * (1.0 / 65535.0)
            dx, dy, dz = x - far_x, y - far_y, z - far_z
            total = total + strength * lax.rsqrt(dx * dx + dy * dy + dz * dz + SOFT)
        near_ref[pl.ds(base, 8), :] = total * (1.0 / list_ref.shape[0])
        return carry

    lax.fori_loop(0, leaf_dev // 8, group, 0)
    own_up.wait()
    from_peers = send(parents_ref.at[pl.ds(0, chips - 1), 0], parents_ref.at[pl.ds(0, chips - 1), 0], 3, other(1))
    from_peers.wait_recv()
    sibling = me + 1 - 2 * core
    pass_on = send(parents_ref.at[:, core], parents_ref.at[:, core], 4, sibling)
    pass_on.start()
    from_peers.wait_send()
    own.wait()
    rest = pl.ds(0, (devices - 1) * cap)
    all_leaves = send(out_ref.at[rest, :], arrived_ref.at[rest, :], 2, other(1))
    all_leaves.wait_recv()
    all_leaves.wait_send()
    pass_on.wait()


def exchange(n_sec, n_sub, rows, charges, p2m, m2m, positions, near_list):
    leaf_dev, panels = charges.shape
    coeffs = p2m.shape[1]
    devices = n_sec * n_sub
    full = leaf_dev + 2 * EDGE
    share = leaf_dev // 8
    return pl.pallas_call(
        functools.partial(exchange_kernel, n_sec, n_sub),
        out_shape=(
            jax.ShapeDtypeStruct((leaf_dev, coeffs), BF16),
            jax.ShapeDtypeStruct((rows.shape[0], coeffs), BF16),
            jax.ShapeDtypeStruct((devices // 2, 2, share, coeffs), BF16),
            jax.ShapeDtypeStruct((leaf_dev, panels), F32),
        ),
        in_specs=[SMEM] + [ANY] * 5,
        out_specs=(VMEM, ANY, ANY, VMEM),
        scratch_shapes=[
            pltpu.VMEM(charges.shape, BF16),
            pltpu.VMEM(p2m.shape, BF16),
            pltpu.VMEM(m2m.shape, BF16),
            pltpu.VMEM(positions.shape, F32),
            pltpu.VMEM(near_list.shape, I32),
            pltpu.VMEM((leaf_dev, coeffs), F32),
            pltpu.VMEM((128, coeffs), F32),
            pltpu.VMEM((rows.shape[0], coeffs), BF16),
            pltpu.VMEM((share, coeffs), BF16),
            pltpu.VMEM((2, 4, EDGE, panels), F32),
            pltpu.VMEM((2, 4, EDGE, panels), F32),
            pltpu.VMEM((full, panels), I32),
            pltpu.VMEM((full, panels), F32),
            pltpu.SemaphoreType.DMA((5,)),
            pltpu.SemaphoreType.DMA((5,)),
            pltpu.SemaphoreType.DMA((5,)),
            pltpu.SemaphoreType.DMA((2,)),
        ],
        compiler_params=pltpu.CompilerParams(vmem_limit_bytes=58 << 20, collective_id=0, has_side_effects=True),
        name="exchange",
    )(rows, charges, p2m, m2m, positions, near_list)


GROUP = 16
QUAD = 4


def far_kernel(
    leaf_list_hbm, parent_list_ref, leaf_types_hbm, parent_types_ref, arrived_hbm, own_hbm, parents_hbm,
    m2l_hbm, l2l_hbm, l2p_hbm, near_hbm, out_ref,
    table, lists, types, tall_a, tall_b, grouped, m2l, total, flat_list, flat_types, square, narrow, l2l_ref, l2p_ref, near_ref,
    index_a, index_b, sems, in_sems,
):
    leaf_dev = out_ref.shape[0]
    boxes, entries = lists.shape
    wide = types.shape[1]
    kinds, coeffs = m2l.shape[0], m2l.shape[2]
    steps = boxes // GROUP
    loads = []
    first = 0
    for source in (arrived_hbm, own_hbm, parents_hbm):
        loads.append((source, narrow.at[pl.ds(first, source.shape[0]), :]))
        first += source.shape[0]
    loads += [(leaf_list_hbm, flat_list), (leaf_types_hbm, flat_types)]
    loads += [(l2l_hbm, l2l_ref), (l2p_hbm, l2p_ref), (near_hbm, near_ref)]
    loads = [pltpu.make_async_copy(source, target, in_sems.at[i]) for i, (source, target) in enumerate(loads)]
    for i in (3, 4, 0, 1, 2):
        loads[i].start()
    weights = pltpu.make_async_copy(m2l_hbm, m2l, sems.at[2])
    weights.start()
    for load in loads[5:]:
        load.start()
    leaf_rows = arrived_hbm.shape[0] + own_hbm.shape[0]
    tall_b[...] = jnp.zeros_like(tall_b)
    lift = 8 - lax.broadcasted_iota(I32, (1, entries), 1) % 8
    loads[3].wait()
    square[pl.ds(0, entries), :] = flat_list[...]
    lists[pl.ds(0, leaf_dev), :] = square[...].T[:, :entries] + lift
    lists[pl.ds(leaf_dev, boxes - leaf_dev), :] = parent_list_ref[...] + (lift + leaf_rows)

    def fetch(step, buffer, which):
        at = pl.multiple_of(step * GROUP, GROUP)
        return pltpu.make_async_copy(lists.at[pl.ds(at, GROUP), :], buffer, sems.at[which])

    fetch(0, index_a, 0).start()
    fetch(1, index_b, 1).start()
    types[...] = jnp.full_like(types, -1)
    loads[4].wait()
    square[pl.ds(0, entries), :] = flat_types[...]
    types[pl.ds(0, leaf_dev), pl.ds(0, entries)] = square[...].T[:, :entries]
    types[pl.ds(leaf_dev, boxes - leaf_dev), pl.ds(0, entries)] = parent_types_ref[...]
    for load in loads[:3]:
        load.wait()
    table[pl.ds(0, 8), :] = jnp.zeros((8, coeffs), F32)
    table[pl.ds(table.shape[0] - 8, 8), :] = jnp.zeros((8, coeffs), F32)
    table[pl.ds(8, narrow.shape[0]), :] = narrow[...].astype(F32)
    kinds_up = tall_a.shape[1] // QUAD - 4
    kind_of = lax.broadcasted_iota(I32, (kinds_up, types.shape[1]), 0)
    sub = lax.broadcasted_iota(I32, (8, coeffs), 0)
    upper = lax.broadcasted_iota(I32, (8, coeffs), 0) >= QUAD

    def spread(index, tall, step):
        for box in range(GROUP):
            kind = types[pl.ds(step * GROUP + box, 1), :]
            onehot = (kind_of == kind).astype(BF16)
            tiles = []
            for v in range(wide // 8):
                tile = None
                for r in range(8):
                    if v * 8 + r < entries:
                        row = table[pl.ds(index[box, v * 8 + r], 8), :]
                        tile = row if tile is None else jnp.where(sub == r, row, tile)
                tiles.append(tile)
            picked = jnp.concatenate(tiles, 0).astype(BF16)
            tall[box // QUAD, pl.ds(8 + box % QUAD, kinds_up, stride=QUAD), :] = jnp.dot(
                onehot, picked, preferred_element_type=F32
            )

    def turn(tall, step):
        at = pl.multiple_of(step * GROUP, GROUP)
        for t in range(kinds):
            pair = [
                jnp.where(upper, tall[2 * h + 1, pl.ds(8 + t * QUAD - QUAD, 8), :], tall[2 * h, pl.ds(8 + t * QUAD, 8), :])
                for h in range(2)
            ]
            grouped[t, pl.ds(at, GROUP), :] = jnp.concatenate(pair, 0).astype(BF16)

    def some(i, carry):
        for half, index, tall, done in ((0, index_a, tall_a, tall_b), (1, index_b, tall_b, tall_a)):
            step = i * 2 + half
            fetch(step, index, half).wait()
            spread(index, tall, step)
            turn(done, jnp.maximum(step - 1, 0))
            fetch(jnp.minimum(step + 2, steps - 2 + half), index, half).start()
        return carry

    lax.fori_loop(0, steps // 2, some, 0)
    for half, index in ((0, index_a), (1, index_b)):
        fetch(steps - 2 + half, index, half).wait()
    turn(tall_b, steps - 1)
    weights.wait()
    for load in loads[5:]:
        load.wait()
    total[...] = jnp.zeros_like(total)
    chunk = 12

    def multiply(first, count):
        left = jnp.concatenate([grouped[first + t] for t in range(count)], axis=1)
        right = m2l[pl.ds(first, count)].reshape(count * coeffs, coeffs)
        total[...] += jnp.dot(left, right, preferred_element_type=F32)

    def several(i, carry):
        multiply(i * chunk, chunk)
        return carry

    lax.fori_loop(0, kinds // chunk, several, 0)
    if kinds % chunk:
        multiply(kinds // chunk * chunk, kinds % chunk)
    parents = boxes - leaf_dev
    parent_local = total[pl.ds(leaf_dev, parents), :].astype(BF16)
    for octant in range(8):
        down = jnp.dot(parent_local, l2l_ref[octant], preferred_element_type=F32)
        total[pl.ds(octant, parents, stride=8), :] += down
    leaf_total = total[pl.ds(0, leaf_dev), :].astype(BF16)
    out_ref[...] = jnp.dot(leaf_total, l2p_ref[...], preferred_element_type=F32) + near_ref[...]


def far_field(leaf_list, parent_list, leaf_types, parent_types, arrived, own, parents, m2l, l2l, l2p, near):
    boxes, entries = leaf_list.shape[0] + parent_list.shape[0], leaf_list.shape[1]
    square = -(-entries // 128) * 128
    kinds, coeffs = m2l.shape[0], m2l.shape[2]
    tables = arrived.shape[0] + own.shape[0] + parents.shape[0]
    wide = -(-entries // 16) * 16
    kinds_up = -(-kinds // 16) * 16
    return pl.pallas_call(
        far_kernel,
        out_shape=jax.ShapeDtypeStruct(near.shape, F32),
        in_specs=[ANY, VMEM, ANY, VMEM] + [ANY] * 7,
        out_specs=VMEM,
        scratch_shapes=[
            pltpu.VMEM((tables + 16, coeffs), F32),
            pltpu.VMEM((boxes, entries), I32),
            pltpu.VMEM((boxes, wide), I32),
            pltpu.VMEM((GROUP // QUAD, kinds_up * QUAD + 4 * QUAD, coeffs), F32),
            pltpu.VMEM((GROUP // QUAD, kinds_up * QUAD + 4 * QUAD, coeffs), F32),
            pltpu.VMEM((kinds, boxes, coeffs), BF16),
            pltpu.VMEM(m2l.shape, BF16),
            pltpu.VMEM((boxes, coeffs), F32),
            pltpu.VMEM((entries, leaf_list.shape[0]), I32),
            pltpu.VMEM((entries, leaf_list.shape[0]), I32),
            pltpu.VMEM((square, leaf_list.shape[0]), I32),
            pltpu.VMEM((tables, coeffs), BF16),
            pltpu.VMEM(l2l.shape, BF16),
            pltpu.VMEM(l2p.shape, BF16),
            pltpu.VMEM(near.shape, F32),
            pltpu.SMEM((GROUP, entries), I32),
            pltpu.SMEM((GROUP, entries), I32),
            pltpu.SemaphoreType.DMA((3,)),
            pltpu.SemaphoreType.DMA((8,)),
        ],
        compiler_params=pltpu.CompilerParams(vmem_limit_bytes=58 << 20),
        name="far",
    )(leaf_list.T, parent_list, leaf_types.T, parent_types, arrived, own, parents, m2l, l2l, l2p, near)


def local(
    charges, positions, p2m, m2m, m2l, l2l, l2p,
    send_rows, send_counts, leaf_list, leaf_types, parent_list, parent_types, near_list,
):
    n_sec, n_sub = lax.axis_size("sec"), lax.axis_size("sub")
    rows = send_rows.reshape(n_sec * n_sub * send_rows.shape[2])
    own, arrived, parents, near = exchange(n_sec, n_sub, rows, charges, p2m, m2m, positions, near_list)
    parents = parents.reshape(parents.shape[0] * parents.shape[1] * parents.shape[2], parents.shape[3])
    return far_field(leaf_list, parent_list, leaf_types, parent_types, arrived, own, parents, m2l, l2l, l2p, near)


def solution(mesh):
    along = P(BOTH, None)
    in_specs = (
        along, P(None, BOTH, None), P(), P(), P(), P(), P(),
        P(BOTH, None, None), along, along, along, along, along, P(None, BOTH, None),
    )
    return jax.shard_map(local, mesh=mesh, in_specs=in_specs, out_specs=along, check_vma=False)
```

```python
import functools

import jax
import jax.numpy as jnp
from jax import lax
from jax.experimental import pallas as pl
from jax.experimental.pallas import tpu as pltpu
from jax.sharding import PartitionSpec as P

RIM = 512
SOFT = 0.0025
BOTH = ("sec", "sub")
F32 = jnp.float32
BF16 = jnp.bfloat16
I32 = jnp.int32
SMEM = pl.BlockSpec(memory_space=pltpu.SMEM)
VMEM = pl.BlockSpec(memory_space=pltpu.VMEM)
ANY = pl.BlockSpec(memory_space=pl.ANY)


Z_SCALE = 2.0**-10
EDGE = 8
STRIDE = 37
MESH = pl.DeviceIdType.MESH


def exchange_kernel(
    n_sec, n_sub, rows_ref, charge_hbm, p2m_hbm, m2m_hbm, pos_hbm, list_hbm, own_ref, arrived_ref, parents_ref, near_ref,
    charge_ref, p2m_ref, m2m_ref, pos_ref, list_ref, wide, block, out_ref, parent_ref,
    edge, halo, xy, zq, in_sems, send_sems, recv_sems, own_sems,
):
    devices = n_sec * n_sub
    me = lax.axis_index("sec") * n_sub + lax.axis_index("sub")
    chip, core = me // 2, me % 2
    chips = devices // 2
    cap = out_ref.shape[0] // devices
    leaf_dev, panels = near_ref.shape

    def place_of(device):
        return (device // n_sub, device % n_sub)

    def other(distance):
        return (me + distance) % devices

    loads = [
        pltpu.make_async_copy(source, target, in_sems.at[i])
        for i, (source, target) in enumerate(
            ((charge_hbm, charge_ref), (p2m_hbm, p2m_ref), (m2m_hbm, m2m_ref), (pos_hbm, pos_ref), (list_hbm, list_ref))
        )
    ]
    for load in loads:
        load.start()
    barrier = pltpu.get_barrier_semaphore()

    def greet(d, carry):
        pl.semaphore_signal(barrier, inc=1, device_id=place_of(other((d * STRIDE) % devices)), device_id_type=MESH)
        return carry

    lax.fori_loop(1, devices, greet, 0)
    for load in loads[:3]:
        load.wait()
    mult = jnp.dot(charge_ref[...], p2m_ref[...], preferred_element_type=F32).astype(BF16)
    own_ref[...] = mult
    wide[...] = mult.astype(F32)
    share = parent_ref.shape[0]
    total = jnp.zeros(parent_ref.shape, F32)
    for octant in range(8):
        child = wide[pl.ds(octant, share, stride=8), :].astype(BF16)
        total = total + jnp.dot(child, m2m_ref[octant], preferred_element_type=F32)
    parent_ref[...] = total.astype(BF16)
    loads[3].wait()
    for side, rows in ((0, pl.ds(leaf_dev - EDGE, EDGE)), (1, pl.ds(0, EDGE))):
        for axis in range(3):
            edge[side, axis] = pos_ref[axis, rows, :]
    charges = charge_ref[...].astype(F32)
    edge[0, 3] = charges[leaf_dev - EDGE :]
    edge[1, 3] = charges[:EDGE]
    pl.semaphore_wait(barrier, devices - 1)

    def send(source, target, which, device):
        return pltpu.make_async_remote_copy(
            src_ref=source, dst_ref=target, send_sem=send_sems.at[which], recv_sem=recv_sems.at[which],
            device_id=place_of(device), device_id_type=MESH,
        )

    def to_side(side):
        return send(edge.at[side], halo.at[side], side, other(1 if side == 0 else devices - 1))

    to_side(0).start()
    to_side(1).start()
    mine = pl.ds(pl.multiple_of(me * cap, cap), cap)

    def give_up(d, carry):
        send(parent_ref, parents_ref.at[chip, core], 3, other((2 * d * STRIDE) % devices)).start()
        return carry

    def give(d, carry):
        device = other((d * STRIDE) % devices)
        send(out_ref.at[pl.ds(pl.multiple_of(device * cap, cap), cap), :], arrived_ref.at[mine, :], 2, device).start()
        return carry

    lax.fori_loop(1, chips, give_up, 0)
    step = block.shape[0]

    def some(g, carry):
        for u in range(step):
            block[pl.ds(u, 1), :] = wide[pl.ds(rows_ref[u % cap, g * (step // cap) + u // cap], 1), :]
        out_ref[pl.ds(pl.multiple_of(g * step, step), step), :] = block[...].astype(BF16)
        return carry

    lax.fori_loop(0, out_ref.shape[0] // step, some, 0)
    lax.fori_loop(1, devices, give, 0)
    own = pltpu.make_async_copy(out_ref.at[mine, :], arrived_ref.at[mine, :], own_sems.at[0])
    own_up = pltpu.make_async_copy(parent_ref, parents_ref.at[chip, core], own_sems.at[1])
    own.start()
    own_up.start()
    loads[4].wait()

    def store(x, y, z, q, first, count):
        whole_x = jnp.round(x * 65535.0).astype(I32) - 32768
        whole_y = jnp.round(y * 65535.0).astype(I32)
        xy[pl.ds(first, count), :] = whole_x * 65536 + whole_y
        zq[pl.ds(first, count), :] = q * (1.0 + (z - 0.5) * Z_SCALE)

    store(pos_ref[0], pos_ref[1], pos_ref[2], charges, EDGE, leaf_dev)
    for side, end, first in ((0, 0, 0), (1, devices - 1, EDGE + leaf_dev)):
        to_side(side).wait()
        strength = halo[side, 3] * jnp.where(me == end, 0.0, 1.0)
        store(halo[side, 0], halo[side, 1], halo[side, 2], strength, first, EDGE)
    lane = lax.broadcasted_iota(I32, (8, panels), 1)
    rim = RIM // panels

    def group(g, carry):
        base = pl.multiple_of(g * 8, 8)
        x = pos_ref[0, pl.ds(base, 8), :]
        y = pos_ref[1, pl.ds(base, 8), :]
        z = pos_ref[2, pl.ds(base, 8), :]
        total = jnp.zeros((8, panels), F32)
        for n in range(list_ref.shape[0]):
            target = list_ref[n, pl.ds(base, 8), :] + lane
            which = target >> 7
            place = target & (panels - 1)
            word = jnp.zeros((8, panels), I32)
            weight = jnp.zeros((8, panels), F32)
            for q in range(2 * rim + 1):
                at = which == q
                rows = pl.ds(base + (EDGE - rim + q), 8)
                word = jnp.where(at, jnp.take_along_axis(xy[rows, :], place, axis=1), word)
                weight = jnp.where(at, jnp.take_along_axis(zq[rows, :], place, axis=1), weight)
            strength = weight.astype(BF16).astype(F32)
            safe = jnp.where(strength == 0.0, 1.0, strength)
            far_z = (weight - strength) / safe * (1.0 / Z_SCALE) + 0.5
            far_x = ((word >> 16) + 32768).astype(F32) * (1.0 / 65535.0)
            far_y = (word & 65535).astype(F32) * (1.0 / 65535.0)
            dx, dy, dz = x - far_x, y - far_y, z - far_z
            total = total + strength * lax.rsqrt(dx * dx + dy * dy + dz * dz + SOFT)
        near_ref[pl.ds(base, 8), :] = total * (1.0 / list_ref.shape[0])
        return carry

    lax.fori_loop(0, leaf_dev // 8, group, 0)
    own_up.wait()
    from_peers = send(parents_ref.at[pl.ds(0, chips - 1), 0], parents_ref.at[pl.ds(0, chips - 1), 0], 3, other(1))
    from_peers.wait_recv()
    sibling = me + 1 - 2 * core
    pass_on = send(parents_ref.at[:, core], parents_ref.at[:, core], 4, sibling)
    pass_on.start()
    from_peers.wait_send()
    own.wait()
    rest = pl.ds(0, (devices - 1) * cap)
    all_leaves = send(out_ref.at[rest, :], arrived_ref.at[rest, :], 2, other(1))
    all_leaves.wait_recv()
    all_leaves.wait_send()
    pass_on.wait()


def exchange(n_sec, n_sub, rows, charges, p2m, m2m, positions, near_list):
    leaf_dev, panels = charges.shape
    coeffs = p2m.shape[1]
    devices = n_sec * n_sub
    full = leaf_dev + 2 * EDGE
    share = leaf_dev // 8
    return pl.pallas_call(
        functools.partial(exchange_kernel, n_sec, n_sub),
        out_shape=(
            jax.ShapeDtypeStruct((leaf_dev, coeffs), BF16),
            jax.ShapeDtypeStruct((rows.size, coeffs), BF16),
            jax.ShapeDtypeStruct((devices // 2, 2, share, coeffs), BF16),
            jax.ShapeDtypeStruct((leaf_dev, panels), F32),
        ),
        in_specs=[SMEM] + [ANY] * 5,
        out_specs=(VMEM, ANY, ANY, VMEM),
        scratch_shapes=[
            pltpu.VMEM(charges.shape, BF16),
            pltpu.VMEM(p2m.shape, BF16),
            pltpu.VMEM(m2m.shape, BF16),
            pltpu.VMEM(positions.shape, F32),
            pltpu.VMEM(near_list.shape, I32),
            pltpu.VMEM((leaf_dev, coeffs), F32),
            pltpu.VMEM((128, coeffs), F32),
            pltpu.VMEM((rows.size, coeffs), BF16),
            pltpu.VMEM((share, coeffs), BF16),
            pltpu.VMEM((2, 4, EDGE, panels), F32),
            pltpu.VMEM((2, 4, EDGE, panels), F32),
            pltpu.VMEM((full, panels), I32),
            pltpu.VMEM((full, panels), F32),
            pltpu.SemaphoreType.DMA((5,)),
            pltpu.SemaphoreType.DMA((5,)),
            pltpu.SemaphoreType.DMA((5,)),
            pltpu.SemaphoreType.DMA((2,)),
        ],
        compiler_params=pltpu.CompilerParams(vmem_limit_bytes=58 << 20, collective_id=0, has_side_effects=True),
        name="exchange",
    )(rows, charges, p2m, m2m, positions, near_list)


GROUP = 16
QUAD = 8


def far_kernel(
    leaf_list_hbm, parent_list_ref, leaf_types_hbm, parent_types_ref, arrived_hbm, own_hbm, parents_hbm,
    m2l_hbm, l2l_hbm, l2p_hbm, near_hbm, out_ref,
    table, lists, types, tall_a, tall_b, grouped, m2l, total, flat_list, flat_types, square, narrow, l2l_ref, l2p_ref, near_ref,
    index_a, index_b, sems, in_sems,
):
    leaf_dev = out_ref.shape[0]
    boxes, entries = lists.shape
    wide = types.shape[1]
    kinds, coeffs = m2l.shape[0], m2l.shape[2]
    steps = boxes // GROUP
    loads = []
    first = 0
    for source in (arrived_hbm, own_hbm, parents_hbm):
        loads.append((source, narrow.at[pl.ds(first, source.shape[0]), :]))
        first += source.shape[0]
    loads += [(leaf_list_hbm, flat_list), (leaf_types_hbm, flat_types)]
    loads += [(l2l_hbm, l2l_ref), (l2p_hbm, l2p_ref), (near_hbm, near_ref)]
    loads = [pltpu.make_async_copy(source, target, in_sems.at[i]) for i, (source, target) in enumerate(loads)]
    for i in (3, 4, 0, 1, 2):
        loads[i].start()
    weights = pltpu.make_async_copy(m2l_hbm, m2l, sems.at[2])
    weights.start()
    for load in loads[5:]:
        load.start()
    leaf_rows = arrived_hbm.shape[0] + own_hbm.shape[0]
    tall_b[...] = jnp.zeros_like(tall_b)
    lift = 8 - lax.broadcasted_iota(I32, (1, entries), 1) % 8
    loads[3].wait()
    square[pl.ds(0, entries), :] = flat_list[...]
    lists[pl.ds(0, leaf_dev), :] = square[...].T[:, :entries] + lift
    lists[pl.ds(leaf_dev, boxes - leaf_dev), :] = parent_list_ref[...] + (lift + leaf_rows)

    def fetch(step, buffer, which):
        at = pl.multiple_of(step * GROUP, GROUP)
        return pltpu.make_async_copy(lists.at[pl.ds(at, GROUP), :], buffer, sems.at[which])

    fetch(0, index_a, 0).start()
    fetch(1, index_b, 1).start()
    types[...] = jnp.full_like(types, -1)
    loads[4].wait()
    square[pl.ds(0, entries), :] = flat_types[...]
    types[pl.ds(0, leaf_dev), pl.ds(0, entries)] = square[...].T[:, :entries]
    types[pl.ds(leaf_dev, boxes - leaf_dev), pl.ds(0, entries)] = parent_types_ref[...]
    for load in loads[:3]:
        load.wait()
    table[pl.ds(0, 8), :] = jnp.zeros((8, coeffs), F32)
    table[pl.ds(table.shape[0] - 8, 8), :] = jnp.zeros((8, coeffs), F32)
    table[pl.ds(8, narrow.shape[0]), :] = narrow[...].astype(F32)
    kinds_up = tall_a.shape[1] // QUAD
    kind_of = lax.broadcasted_iota(I32, (kinds_up, types.shape[1]), 0)
    sub = lax.broadcasted_iota(I32, (8, coeffs), 0)

    def spread(index, tall, step):
        for box in range(GROUP):
            kind = types[pl.ds(step * GROUP + box, 1), :]
            onehot = (kind_of == kind).astype(BF16)
            tiles = []
            for v in range(wide // 8):
                tile = None
                for r in range(8):
                    if v * 8 + r < entries:
                        row = table[pl.ds(index[box, v * 8 + r], 8), :]
                        tile = row if tile is None else jnp.where(sub == r, row, tile)
                tiles.append(tile)
            picked = jnp.concatenate(tiles, 0).astype(BF16)
            tall[box // QUAD, pl.ds(box % QUAD, kinds_up, stride=QUAD), :] = jnp.dot(
                onehot, picked, preferred_element_type=F32
            )

    def turn(tall, step):
        at = pl.multiple_of(step * GROUP, GROUP)
        for t in range(kinds):
            pair = [tall[h, pl.ds(t * QUAD, QUAD), :] for h in range(GROUP // QUAD)]
            grouped[t, pl.ds(at, GROUP), :] = jnp.concatenate(pair, 0).astype(BF16)

    def some(i, carry):
        for half, index, tall, done in ((0, index_a, tall_a, tall_b), (1, index_b, tall_b, tall_a)):
            step = i * 2 + half
            fetch(step, index, half).wait()
            spread(index, tall, step)
            turn(done, jnp.maximum(step - 1, 0))
            fetch(jnp.minimum(step + 2, steps - 2 + half), index, half).start()
        return carry

    lax.fori_loop(0, steps // 2, some, 0)
    for half, index in ((0, index_a), (1, index_b)):
        fetch(steps - 2 + half, index, half).wait()
    turn(tall_b, steps - 1)
    weights.wait()
    for load in loads[5:]:
        load.wait()
    total[...] = jnp.zeros_like(total)
    chunk = 28

    def multiply(first, count):
        left = jnp.concatenate([grouped[first + t] for t in range(count)], axis=1)
        right = m2l[pl.ds(first, count)].reshape(count * coeffs, coeffs)
        total[...] += jnp.dot(left, right, preferred_element_type=F32)

    def several(i, carry):
        multiply(i * chunk, chunk)
        return carry

    lax.fori_loop(0, kinds // chunk, several, 0)
    if kinds % chunk:
        multiply(kinds // chunk * chunk, kinds % chunk)
    parents = boxes - leaf_dev
    parent_local = total[pl.ds(leaf_dev, parents), :].astype(BF16)
    for octant in range(8):
        down = jnp.dot(parent_local, l2l_ref[octant], preferred_element_type=F32)
        total[pl.ds(octant, parents, stride=8), :] += down
    leaf_total = total[pl.ds(0, leaf_dev), :].astype(BF16)
    out_ref[...] = jnp.dot(leaf_total, l2p_ref[...], preferred_element_type=F32) + near_ref[...]


def far_field(leaf_list, parent_list, leaf_types, parent_types, arrived, own, parents, m2l, l2l, l2p, near):
    boxes, entries = leaf_list.shape[0] + parent_list.shape[0], leaf_list.shape[1]
    square = -(-entries // 128) * 128
    kinds, coeffs = m2l.shape[0], m2l.shape[2]
    tables = arrived.shape[0] + own.shape[0] + parents.shape[0]
    wide = -(-entries // 16) * 16
    kinds_up = -(-kinds // 16) * 16
    return pl.pallas_call(
        far_kernel,
        out_shape=jax.ShapeDtypeStruct(near.shape, F32),
        in_specs=[ANY, VMEM, ANY, VMEM] + [ANY] * 7,
        out_specs=VMEM,
        scratch_shapes=[
            pltpu.VMEM((tables + 16, coeffs), F32),
            pltpu.VMEM((boxes, entries), I32),
            pltpu.VMEM((boxes, wide), I32),
            pltpu.VMEM((GROUP // QUAD, kinds_up * QUAD, coeffs), F32),
            pltpu.VMEM((GROUP // QUAD, kinds_up * QUAD, coeffs), F32),
            pltpu.VMEM((kinds, boxes, coeffs), BF16),
            pltpu.VMEM(m2l.shape, BF16),
            pltpu.VMEM((boxes, coeffs), F32),
            pltpu.VMEM((entries, leaf_list.shape[0]), I32),
            pltpu.VMEM((entries, leaf_list.shape[0]), I32),
            pltpu.VMEM((square, leaf_list.shape[0]), I32),
            pltpu.VMEM((tables, coeffs), BF16),
            pltpu.VMEM(l2l.shape, BF16),
            pltpu.VMEM(l2p.shape, BF16),
            pltpu.VMEM(near.shape, F32),
            pltpu.SMEM((GROUP, entries), I32),
            pltpu.SMEM((GROUP, entries), I32),
            pltpu.SemaphoreType.DMA((3,)),
            pltpu.SemaphoreType.DMA((8,)),
        ],
        compiler_params=pltpu.CompilerParams(vmem_limit_bytes=58 << 20),
        name="far",
    )(leaf_list.T, parent_list, leaf_types.T, parent_types, arrived, own, parents, m2l, l2l, l2p, near)


def local(
    charges, positions, p2m, m2m, m2l, l2l, l2p,
    send_rows, send_counts, leaf_list, leaf_types, parent_list, parent_types, near_list,
):
    n_sec, n_sub = lax.axis_size("sec"), lax.axis_size("sub")
    own, arrived, parents, near = exchange(n_sec, n_sub, send_rows[0].T, charges, p2m, m2m, positions, near_list)
    parents = parents.reshape(parents.shape[0] * parents.shape[1] * parents.shape[2], parents.shape[3])
    return far_field(leaf_list, parent_list, leaf_types, parent_types, arrived, own, parents, m2l, l2l, l2p, near)


def solution(mesh):
    along = P(BOTH, None)
    in_specs = (
        along, P(None, BOTH, None), P(), P(), P(), P(), P(),
        P(BOTH, None, None), along, along, along, along, along, P(None, BOTH, None),
    )
    return jax.shard_map(local, mesh=mesh, in_specs=in_specs, out_specs=along, check_vma=False)
```

```python
import functools

import jax
import jax.numpy as jnp
from jax import lax
from jax.experimental import pallas as pl
from jax.experimental.pallas import tpu as pltpu
from jax.sharding import PartitionSpec as P

RIM = 512
SOFT = 0.0025
BOTH = ("sec", "sub")
F32 = jnp.float32
BF16 = jnp.bfloat16
I32 = jnp.int32
SMEM = pl.BlockSpec(memory_space=pltpu.SMEM)
VMEM = pl.BlockSpec(memory_space=pltpu.VMEM)
ANY = pl.BlockSpec(memory_space=pl.ANY)


Z_SCALE = 2.0**-10
EDGE = 8
STRIDE = 37
MESH = pl.DeviceIdType.MESH


def exchange_kernel(
    n_sec, n_sub, rows_ref, charge_hbm, p2m_hbm, m2m_hbm, pos_hbm, list_hbm, own_ref, arrived_ref, parents_ref, near_ref,
    charge_ref, p2m_ref, m2m_ref, pos_ref, list_ref, wide, block, out_ref, parent_ref,
    edge, halo, xy, zq, in_sems, send_sems, recv_sems, own_sems,
):
    devices = n_sec * n_sub
    me = lax.axis_index("sec") * n_sub + lax.axis_index("sub")
    chip, core = me // 2, me % 2
    chips = devices // 2
    cap = out_ref.shape[0] // devices
    leaf_dev, panels = near_ref.shape

    def place_of(device):
        return (device // n_sub, device % n_sub)

    def other(distance):
        return (me + distance) % devices

    loads = [
        pltpu.make_async_copy(source, target, in_sems.at[i])
        for i, (source, target) in enumerate(
            ((charge_hbm, charge_ref), (p2m_hbm, p2m_ref), (m2m_hbm, m2m_ref), (pos_hbm, pos_ref), (list_hbm, list_ref))
        )
    ]
    for load in loads:
        load.start()
    barrier = pltpu.get_barrier_semaphore()

    def greet(d, carry):
        pl.semaphore_signal(barrier, inc=1, device_id=place_of(other((d * STRIDE) % devices)), device_id_type=MESH)
        return carry

    lax.fori_loop(1, devices, greet, 0)
    for load in loads[:3]:
        load.wait()
    mult = jnp.dot(charge_ref[...], p2m_ref[...], preferred_element_type=F32).astype(BF16)
    own_ref[...] = mult
    wide[...] = mult.astype(F32)
    share = parent_ref.shape[0]
    total = jnp.zeros(parent_ref.shape, F32)
    for octant in range(8):
        child = wide[pl.ds(octant, share, stride=8), :].astype(BF16)
        total = total + jnp.dot(child, m2m_ref[octant], preferred_element_type=F32)
    parent_ref[...] = total.astype(BF16)
    step = block.shape[0]

    def some(g, carry):
        rows = rows_ref.at[pl.ds(g * step, step)]
        for u in range(step):
            block[pl.ds(u, 1), :] = wide[pl.ds(rows[u], 1), :]
        out_ref[pl.ds(pl.multiple_of(g * step, step), step), :] = block[...].astype(BF16)
        return carry

    lax.fori_loop(0, out_ref.shape[0] // step, some, 0)
    loads[3].wait()
    for side, rows in ((0, pl.ds(leaf_dev - EDGE, EDGE)), (1, pl.ds(0, EDGE))):
        for axis in range(3):
            edge[side, axis] = pos_ref[axis, rows, :]
    charges = charge_ref[...].astype(F32)
    edge[0, 3] = charges[leaf_dev - EDGE :]
    edge[1, 3] = charges[:EDGE]
    pl.semaphore_wait(barrier, devices - 1)

    def send(source, target, which, device):
        return pltpu.make_async_remote_copy(
            src_ref=source, dst_ref=target, send_sem=send_sems.at[which], recv_sem=recv_sems.at[which],
            device_id=place_of(device), device_id_type=MESH,
        )

    def to_side(side):
        return send(edge.at[side], halo.at[side], side, other(1 if side == 0 else devices - 1))

    to_side(0).start()
    to_side(1).start()
    mine = pl.ds(pl.multiple_of(me * cap, cap), cap)

    def give_up(d, carry):
        send(parent_ref, parents_ref.at[chip, core], 3, other((2 * d * STRIDE) % devices)).start()
        return carry

    def give(d, carry):
        device = other((d * STRIDE) % devices)
        send(out_ref.at[pl.ds(pl.multiple_of(device * cap, cap), cap), :], arrived_ref.at[mine, :], 2, device).start()
        return carry

    lax.fori_loop(1, chips, give_up, 0)
    lax.fori_loop(1, devices, give, 0)
    own = pltpu.make_async_copy(out_ref.at[mine, :], arrived_ref.at[mine, :], own_sems.at[0])
    own_up = pltpu.make_async_copy(parent_ref, parents_ref.at[chip, core], own_sems.at[1])
    own.start()
    own_up.start()
    loads[4].wait()

    def store(x, y, z, q, first, count):
        whole_x = jnp.round(x * 65535.0).astype(I32) - 32768
        whole_y = jnp.round(y * 65535.0).astype(I32)
        xy[pl.ds(first, count), :] = whole_x * 65536 + whole_y
        zq[pl.ds(first, count), :] = q * (1.0 + (z - 0.5) * Z_SCALE)

    store(pos_ref[0], pos_ref[1], pos_ref[2], charges, EDGE, leaf_dev)
    for side, end, first in ((0, 0, 0), (1, devices - 1, EDGE + leaf_dev)):
        to_side(side).wait()
        strength = halo[side, 3] * jnp.where(me == end, 0.0, 1.0)
        store(halo[side, 0], halo[side, 1], halo[side, 2], strength, first, EDGE)
    lane = lax.broadcasted_iota(I32, (8, panels), 1)
    rim = RIM // panels

    def group(g, carry):
        base = pl.multiple_of(g * 8, 8)
        x = pos_ref[0, pl.ds(base, 8), :]
        y = pos_ref[1, pl.ds(base, 8), :]
        z = pos_ref[2, pl.ds(base, 8), :]
        total = jnp.zeros((8, panels), F32)
        for n in range(list_ref.shape[0]):
            target = list_ref[n, pl.ds(base, 8), :] + lane
            which = target >> 7
            place = target & (panels - 1)
            word = jnp.zeros((8, panels), I32)
            weight = jnp.zeros((8, panels), F32)
            for q in range(2 * rim + 1):
                at = which == q
                rows = pl.ds(base + (EDGE - rim + q), 8)
                word = jnp.where(at, jnp.take_along_axis(xy[rows, :], place, axis=1), word)
                weight = jnp.where(at, jnp.take_along_axis(zq[rows, :], place, axis=1), weight)
            strength = weight.astype(BF16).astype(F32)
            safe = jnp.where(strength == 0.0, 1.0, strength)
            far_z = (weight - strength) / safe * (1.0 / Z_SCALE) + 0.5
            far_x = ((word >> 16) + 32768).astype(F32) * (1.0 / 65535.0)
            far_y = (word & 65535).astype(F32) * (1.0 / 65535.0)
            dx, dy, dz = x - far_x, y - far_y, z - far_z
            total = total + strength * lax.rsqrt(dx * dx + dy * dy + dz * dz + SOFT)
        near_ref[pl.ds(base, 8), :] = total * (1.0 / list_ref.shape[0])
        return carry

    lax.fori_loop(0, leaf_dev // 8, group, 0)
    own_up.wait()
    from_peers = send(parents_ref.at[pl.ds(0, chips - 1), 0], parents_ref.at[pl.ds(0, chips - 1), 0], 3, other(1))
    from_peers.wait_recv()
    sibling = me + 1 - 2 * core
    pass_on = send(parents_ref.at[:, core], parents_ref.at[:, core], 4, sibling)
    pass_on.start()
    from_peers.wait_send()
    own.wait()
    rest = pl.ds(0, (devices - 1) * cap)
    all_leaves = send(out_ref.at[rest, :], arrived_ref.at[rest, :], 2, other(1))
    all_leaves.wait_recv()
    all_leaves.wait_send()
    pass_on.wait()


def exchange(n_sec, n_sub, rows, charges, p2m, m2m, positions, near_list):
    leaf_dev, panels = charges.shape
    coeffs = p2m.shape[1]
    devices = n_sec * n_sub
    full = leaf_dev + 2 * EDGE
    share = leaf_dev // 8
    return pl.pallas_call(
        functools.partial(exchange_kernel, n_sec, n_sub),
        out_shape=(
            jax.ShapeDtypeStruct((leaf_dev, coeffs), BF16),
            jax.ShapeDtypeStruct((rows.shape[0], coeffs), BF16),
            jax.ShapeDtypeStruct((devices // 2, 2, share, coeffs), BF16),
            jax.ShapeDtypeStruct((leaf_dev, panels), F32),
        ),
        in_specs=[SMEM] + [ANY] * 5,
        out_specs=(VMEM, ANY, ANY, VMEM),
        scratch_shapes=[
            pltpu.VMEM(charges.shape, BF16),
            pltpu.VMEM(p2m.shape, BF16),
            pltpu.VMEM(m2m.shape, BF16),
            pltpu.VMEM(positions.shape, F32),
            pltpu.VMEM(near_list.shape, I32),
            pltpu.VMEM((leaf_dev, coeffs), F32),
            pltpu.VMEM((128, coeffs), F32),
            pltpu.VMEM((rows.shape[0], coeffs), BF16),
            pltpu.VMEM((share, coeffs), BF16),
            pltpu.VMEM((2, 4, EDGE, panels), F32),
            pltpu.VMEM((2, 4, EDGE, panels), F32),
            pltpu.VMEM((full, panels), I32),
            pltpu.VMEM((full, panels), F32),
            pltpu.SemaphoreType.DMA((5,)),
            pltpu.SemaphoreType.DMA((5,)),
            pltpu.SemaphoreType.DMA((5,)),
            pltpu.SemaphoreType.DMA((2,)),
        ],
        compiler_params=pltpu.CompilerParams(vmem_limit_bytes=58 << 20, collective_id=0, has_side_effects=True),
        name="exchange",
    )(rows, charges, p2m, m2m, positions, near_list)


GROUP = 16
QUAD = 8


def far_kernel(
    leaf_list_hbm, parent_list_ref, leaf_types_hbm, parent_types_ref, arrived_hbm, own_hbm, parents_hbm,
    m2l_hbm, l2l_hbm, l2p_hbm, near_hbm, out_ref,
    table, lists, types, tall_a, tall_b, grouped, m2l, total, flat_list, flat_types, square, narrow, l2l_ref, l2p_ref, near_ref,
    index_a, index_b, sems, in_sems,
):
    leaf_dev = out_ref.shape[0]
    boxes, entries = lists.shape
    wide = types.shape[1]
    kinds, coeffs = m2l.shape[0], m2l.shape[2]
    steps = boxes // GROUP
    loads = []
    first = 0
    for source in (arrived_hbm, own_hbm, parents_hbm):
        loads.append((source, narrow.at[pl.ds(first, source.shape[0]), :]))
        first += source.shape[0]
    loads += [(leaf_list_hbm, flat_list), (leaf_types_hbm, flat_types)]
    loads += [(l2l_hbm, l2l_ref), (l2p_hbm, l2p_ref), (near_hbm, near_ref)]
    loads = [pltpu.make_async_copy(source, target, in_sems.at[i]) for i, (source, target) in enumerate(loads)]
    for i in (3, 4, 0, 1, 2):
        loads[i].start()
    weights = pltpu.make_async_copy(m2l_hbm, m2l, sems.at[2])
    weights.start()
    for load in loads[5:]:
        load.start()
    leaf_rows = arrived_hbm.shape[0] + own_hbm.shape[0]
    tall_b[...] = jnp.zeros_like(tall_b)
    lift = 8 - lax.broadcasted_iota(I32, (1, entries), 1) % 8
    loads[3].wait()
    square[pl.ds(0, entries), :] = flat_list[...]
    lists[pl.ds(0, leaf_dev), :] = square[...].T[:, :entries] + lift
    lists[pl.ds(leaf_dev, boxes - leaf_dev), :] = parent_list_ref[...] + (lift + leaf_rows)

    def fetch(step, buffer, which):
        at = pl.multiple_of(step * GROUP, GROUP)
        return pltpu.make_async_copy(lists.at[pl.ds(at, GROUP), :], buffer, sems.at[which])

    fetch(0, index_a, 0).start()
    fetch(1, index_b, 1).start()
    types[...] = jnp.full_like(types, -1)
    loads[4].wait()
    square[pl.ds(0, entries), :] = flat_types[...]
    types[pl.ds(0, leaf_dev), pl.ds(0, entries)] = square[...].T[:, :entries]
    types[pl.ds(leaf_dev, boxes - leaf_dev), pl.ds(0, entries)] = parent_types_ref[...]
    for load in loads[:3]:
        load.wait()
    table[pl.ds(0, 8), :] = jnp.zeros((8, coeffs), F32)
    table[pl.ds(table.shape[0] - 8, 8), :] = jnp.zeros((8, coeffs), F32)
    table[pl.ds(8, narrow.shape[0]), :] = narrow[...].astype(F32)
    kinds_up = tall_a.shape[1] // QUAD
    kind_of = lax.broadcasted_iota(I32, (kinds_up, types.shape[1]), 0)
    sub = lax.broadcasted_iota(I32, (8, coeffs), 0)

    def spread(index, tall, step):
        for box in range(GROUP):
            kind = types[pl.ds(step * GROUP + box, 1), :]
            onehot = (kind_of == kind).astype(BF16)
            tiles = []
            for v in range(wide // 8):
                tile = None
                for r in range(8):
                    if v * 8 + r < entries:
                        row = table[pl.ds(index[box, v * 8 + r], 8), :]
                        tile = row if tile is None else jnp.where(sub == r, row, tile)
                tiles.append(tile)
            picked = jnp.concatenate(tiles, 0).astype(BF16)
            tall[box // QUAD, pl.ds(box % QUAD, kinds_up, stride=QUAD), :] = jnp.dot(
                onehot, picked, preferred_element_type=F32
            )

    def turn(tall, step):
        at = pl.multiple_of(step * GROUP, GROUP)
        for t in range(kinds):
            pair = [tall[h, pl.ds(t * QUAD, QUAD), :] for h in range(GROUP // QUAD)]
            grouped[t, pl.ds(at, GROUP), :] = jnp.concatenate(pair, 0).astype(BF16)

    def some(i, carry):
        for half, index, tall, done in ((0, index_a, tall_a, tall_b), (1, index_b, tall_b, tall_a)):
            step = i * 2 + half
            fetch(step, index, half).wait()
            spread(index, tall, step)
            turn(done, jnp.maximum(step - 1, 0))
            fetch(jnp.minimum(step + 2, steps - 2 + half), index, half).start()
        return carry

    lax.fori_loop(0, steps // 2, some, 0)
    for half, index in ((0, index_a), (1, index_b)):
        fetch(steps - 2 + half, index, half).wait()
    turn(tall_b, steps - 1)
    weights.wait()
    for load in loads[5:]:
        load.wait()
    total[...] = jnp.zeros_like(total)
    chunk = 28

    def multiply(first, count):
        left = jnp.concatenate([grouped[first + t] for t in range(count)], axis=1)
        right = m2l[pl.ds(first, count)].reshape(count * coeffs, coeffs)
        total[...] += jnp.dot(left, right, preferred_element_type=F32)

    def several(i, carry):
        multiply(i * chunk, chunk)
        return carry

    lax.fori_loop(0, kinds // chunk, several, 0)
    if kinds % chunk:
        multiply(kinds // chunk * chunk, kinds % chunk)
    parents = boxes - leaf_dev
    parent_local = total[pl.ds(leaf_dev, parents), :].astype(BF16)
    for octant in range(8):
        down = jnp.dot(parent_local, l2l_ref[octant], preferred_element_type=F32)
        total[pl.ds(octant, parents, stride=8), :] += down
    leaf_total = total[pl.ds(0, leaf_dev), :].astype(BF16)
    out_ref[...] = jnp.dot(leaf_total, l2p_ref[...], preferred_element_type=F32) + near_ref[...]


def far_field(leaf_list, parent_list, leaf_types, parent_types, arrived, own, parents, m2l, l2l, l2p, near):
    boxes, entries = leaf_list.shape[0] + parent_list.shape[0], leaf_list.shape[1]
    square = -(-entries // 128) * 128
    kinds, coeffs = m2l.shape[0], m2l.shape[2]
    tables = arrived.shape[0] + own.shape[0] + parents.shape[0]
    wide = -(-entries // 16) * 16
    kinds_up = -(-kinds // 16) * 16
    return pl.pallas_call(
        far_kernel,
        out_shape=jax.ShapeDtypeStruct(near.shape, F32),
        in_specs=[ANY, VMEM, ANY, VMEM] + [ANY] * 7,
        out_specs=VMEM,
        scratch_shapes=[
            pltpu.VMEM((tables + 16, coeffs), F32),
            pltpu.VMEM((boxes, entries), I32),
            pltpu.VMEM((boxes, wide), I32),
            pltpu.VMEM((GROUP // QUAD, kinds_up * QUAD, coeffs), F32),
            pltpu.VMEM((GROUP // QUAD, kinds_up * QUAD, coeffs), F32),
            pltpu.VMEM((kinds, boxes, coeffs), BF16),
            pltpu.VMEM(m2l.shape, BF16),
            pltpu.VMEM((boxes, coeffs), F32),
            pltpu.VMEM((entries, leaf_list.shape[0]), I32),
            pltpu.VMEM((entries, leaf_list.shape[0]), I32),
            pltpu.VMEM((square, leaf_list.shape[0]), I32),
            pltpu.VMEM((tables, coeffs), BF16),
            pltpu.VMEM(l2l.shape, BF16),
            pltpu.VMEM(l2p.shape, BF16),
            pltpu.VMEM(near.shape, F32),
            pltpu.SMEM((GROUP, entries), I32),
            pltpu.SMEM((GROUP, entries), I32),
            pltpu.SemaphoreType.DMA((3,)),
            pltpu.SemaphoreType.DMA((8,)),
        ],
        compiler_params=pltpu.CompilerParams(vmem_limit_bytes=58 << 20),
        name="far",
    )(leaf_list.T, parent_list, leaf_types.T, parent_types, arrived, own, parents, m2l, l2l, l2p, near)


def local(
    charges, positions, p2m, m2m, m2l, l2l, l2p,
    send_rows, send_counts, leaf_list, leaf_types, parent_list, parent_types, near_list,
):
    n_sec, n_sub = lax.axis_size("sec"), lax.axis_size("sub")
    rows = send_rows.reshape(n_sec * n_sub * send_rows.shape[2])
    own, arrived, parents, near = exchange(n_sec, n_sub, rows, charges, p2m, m2m, positions, near_list)
    parents = parents.reshape(parents.shape[0] * parents.shape[1] * parents.shape[2], parents.shape[3])
    return far_field(leaf_list, parent_list, leaf_types, parent_types, arrived, own, parents, m2l, l2l, l2p, near)


def solution(mesh):
    along = P(BOTH, None)
    in_specs = (
        along, P(None, BOTH, None), P(), P(), P(), P(), P(),
        P(BOTH, None, None), along, along, along, along, along, P(None, BOTH, None),
    )
    return jax.shard_map(local, mesh=mesh, in_specs=in_specs, out_specs=along, check_vma=False)
```

```python
import functools

import jax
import jax.numpy as jnp
from jax import lax
from jax.experimental import pallas as pl
from jax.experimental.pallas import tpu as pltpu
from jax.sharding import PartitionSpec as P

RIM = 512
SOFT = 0.0025
BOTH = ("sec", "sub")
F32 = jnp.float32
BF16 = jnp.bfloat16
I32 = jnp.int32
SMEM = pl.BlockSpec(memory_space=pltpu.SMEM)
VMEM = pl.BlockSpec(memory_space=pltpu.VMEM)
ANY = pl.BlockSpec(memory_space=pl.ANY)


Z_SCALE = 2.0**-10
EDGE = 8
STRIDE = 37
MESH = pl.DeviceIdType.MESH


def exchange_kernel(
    n_sec, n_sub, rows_ref, charge_hbm, p2m_hbm, m2m_hbm, pos_hbm, list_hbm, own_ref, arrived_ref, parents_ref, near_ref,
    charge_ref, p2m_ref, m2m_ref, pos_ref, list_ref, wide, block, out_ref, parent_ref,
    edge, halo, xy, zq, in_sems, send_sems, recv_sems, own_sems,
):
    devices = n_sec * n_sub
    me = lax.axis_index("sec") * n_sub + lax.axis_index("sub")
    chip, core = me // 2, me % 2
    chips = devices // 2
    cap = out_ref.shape[0] // devices
    leaf_dev, panels = near_ref.shape

    def place_of(device):
        return (device // n_sub, device % n_sub)

    def other(distance):
        return (me + distance) % devices

    loads = [
        pltpu.make_async_copy(source, target, in_sems.at[i])
        for i, (source, target) in enumerate(
            ((charge_hbm, charge_ref), (p2m_hbm, p2m_ref), (m2m_hbm, m2m_ref), (pos_hbm, pos_ref), (list_hbm, list_ref))
        )
    ]
    for load in loads:
        load.start()
    barrier = pltpu.get_barrier_semaphore()

    def greet(d, carry):
        pl.semaphore_signal(barrier, inc=1, device_id=place_of(other((d * STRIDE) % devices)), device_id_type=MESH)
        return carry

    lax.fori_loop(1, devices, greet, 0)
    for load in loads[:3]:
        load.wait()
    mult = jnp.dot(charge_ref[...], p2m_ref[...], preferred_element_type=F32).astype(BF16)
    own_ref[...] = mult
    wide[...] = mult.astype(F32)
    share = parent_ref.shape[0]
    total = jnp.zeros(parent_ref.shape, F32)
    for octant in range(8):
        child = wide[pl.ds(octant, share, stride=8), :].astype(BF16)
        total = total + jnp.dot(child, m2m_ref[octant], preferred_element_type=F32)
    parent_ref[...] = total.astype(BF16)
    step = block.shape[0]

    def some(g, carry):
        for u in range(step):
            block[pl.ds(u, 1), :] = wide[pl.ds(rows_ref[u % cap, g * (step // cap) + u // cap], 1), :]
        out_ref[pl.ds(pl.multiple_of(g * step, step), step), :] = block[...].astype(BF16)
        return carry

    lax.fori_loop(0, out_ref.shape[0] // step, some, 0)
    loads[3].wait()
    for side, rows in ((0, pl.ds(leaf_dev - EDGE, EDGE)), (1, pl.ds(0, EDGE))):
        for axis in range(3):
            edge[side, axis] = pos_ref[axis, rows, :]
    charges = charge_ref[...].astype(F32)
    edge[0, 3] = charges[leaf_dev - EDGE :]
    edge[1, 3] = charges[:EDGE]
    pl.semaphore_wait(barrier, devices - 1)

    def send(source, target, which, device):
        return pltpu.make_async_remote_copy(
            src_ref=source, dst_ref=target, send_sem=send_sems.at[which], recv_sem=recv_sems.at[which],
            device_id=place_of(device), device_id_type=MESH,
        )

    def to_side(side):
        return send(edge.at[side], halo.at[side], side, other(1 if side == 0 else devices - 1))

    to_side(0).start()
    to_side(1).start()
    mine = pl.ds(pl.multiple_of(me * cap, cap), cap)

    def give_up(d, carry):
        send(parent_ref, parents_ref.at[chip, core], 3, other((2 * d * STRIDE) % devices)).start()
        return carry

    def give(d, carry):
        device = other((d * STRIDE) % devices)
        send(out_ref.at[pl.ds(pl.multiple_of(device * cap, cap), cap), :], arrived_ref.at[mine, :], 2, device).start()
        return carry

    lax.fori_loop(1, chips, give_up, 0)
    lax.fori_loop(1, devices, give, 0)
    own = pltpu.make_async_copy(out_ref.at[mine, :], arrived_ref.at[mine, :], own_sems.at[0])
    own_up = pltpu.make_async_copy(parent_ref, parents_ref.at[chip, core], own_sems.at[1])
    own.start()
    own_up.start()
    loads[4].wait()

    def store(x, y, z, q, first, count):
        whole_x = jnp.round(x * 65535.0).astype(I32) - 32768
        whole_y = jnp.round(y * 65535.0).astype(I32)
        xy[pl.ds(first, count), :] = whole_x * 65536 + whole_y
        zq[pl.ds(first, count), :] = q * (1.0 + (z - 0.5) * Z_SCALE)

    store(pos_ref[0], pos_ref[1], pos_ref[2], charges, EDGE, leaf_dev)
    for side, end, first in ((0, 0, 0), (1, devices - 1, EDGE + leaf_dev)):
        to_side(side).wait()
        strength = halo[side, 3] * jnp.where(me == end, 0.0, 1.0)
        store(halo[side, 0], halo[side, 1], halo[side, 2], strength, first, EDGE)
    lane = lax.broadcasted_iota(I32, (8, panels), 1)
    rim = RIM // panels

    def group(g, carry):
        base = pl.multiple_of(g * 8, 8)
        x = pos_ref[0, pl.ds(base, 8), :]
        y = pos_ref[1, pl.ds(base, 8), :]
        z = pos_ref[2, pl.ds(base, 8), :]
        total = jnp.zeros((8, panels), F32)
        for n in range(list_ref.shape[0]):
            target = list_ref[n, pl.ds(base, 8), :] + lane
            which = target >> 7
            place = target & (panels - 1)
            word = jnp.zeros((8, panels), I32)
            weight = jnp.zeros((8, panels), F32)
            for q in range(2 * rim + 1):
                at = which == q
                rows = pl.ds(base + (EDGE - rim + q), 8)
                word = jnp.where(at, jnp.take_along_axis(xy[rows, :], place, axis=1), word)
                weight = jnp.where(at, jnp.take_along_axis(zq[rows, :], place, axis=1), weight)
            strength = weight.astype(BF16).astype(F32)
            safe = jnp.where(strength == 0.0, 1.0, strength)
            far_z = (weight - strength) / safe * (1.0 / Z_SCALE) + 0.5
            far_x = ((word >> 16) + 32768).astype(F32) * (1.0 / 65535.0)
            far_y = (word & 65535).astype(F32) * (1.0 / 65535.0)
            dx, dy, dz = x - far_x, y - far_y, z - far_z
            total = total + strength * lax.rsqrt(dx * dx + dy * dy + dz * dz + SOFT)
        near_ref[pl.ds(base, 8), :] = total * (1.0 / list_ref.shape[0])
        return carry

    lax.fori_loop(0, leaf_dev // 8, group, 0)
    own_up.wait()
    from_peers = send(parents_ref.at[pl.ds(0, chips - 1), 0], parents_ref.at[pl.ds(0, chips - 1), 0], 3, other(1))
    from_peers.wait_recv()
    sibling = me + 1 - 2 * core
    pass_on = send(parents_ref.at[:, core], parents_ref.at[:, core], 4, sibling)
    pass_on.start()
    from_peers.wait_send()
    own.wait()
    rest = pl.ds(0, (devices - 1) * cap)
    all_leaves = send(out_ref.at[rest, :], arrived_ref.at[rest, :], 2, other(1))
    all_leaves.wait_recv()
    all_leaves.wait_send()
    pass_on.wait()


def exchange(n_sec, n_sub, rows, charges, p2m, m2m, positions, near_list):
    leaf_dev, panels = charges.shape
    coeffs = p2m.shape[1]
    devices = n_sec * n_sub
    full = leaf_dev + 2 * EDGE
    share = leaf_dev // 8
    return pl.pallas_call(
        functools.partial(exchange_kernel, n_sec, n_sub),
        out_shape=(
            jax.ShapeDtypeStruct((leaf_dev, coeffs), BF16),
            jax.ShapeDtypeStruct((rows.size, coeffs), BF16),
            jax.ShapeDtypeStruct((devices // 2, 2, share, coeffs), BF16),
            jax.ShapeDtypeStruct((leaf_dev, panels), F32),
        ),
        in_specs=[SMEM] + [ANY] * 5,
        out_specs=(VMEM, ANY, ANY, VMEM),
        scratch_shapes=[
            pltpu.VMEM(charges.shape, BF16),
            pltpu.VMEM(p2m.shape, BF16),
            pltpu.VMEM(m2m.shape, BF16),
            pltpu.VMEM(positions.shape, F32),
            pltpu.VMEM(near_list.shape, I32),
            pltpu.VMEM((leaf_dev, coeffs), F32),
            pltpu.VMEM((128, coeffs), F32),
            pltpu.VMEM((rows.size, coeffs), BF16),
            pltpu.VMEM((share, coeffs), BF16),
            pltpu.VMEM((2, 4, EDGE, panels), F32),
            pltpu.VMEM((2, 4, EDGE, panels), F32),
            pltpu.VMEM((full, panels), I32),
            pltpu.VMEM((full, panels), F32),
            pltpu.SemaphoreType.DMA((5,)),
            pltpu.SemaphoreType.DMA((5,)),
            pltpu.SemaphoreType.DMA((5,)),
            pltpu.SemaphoreType.DMA((2,)),
        ],
        compiler_params=pltpu.CompilerParams(vmem_limit_bytes=58 << 20, collective_id=0, has_side_effects=True),
        name="exchange",
    )(rows, charges, p2m, m2m, positions, near_list)


GROUP = 16
QUAD = 8


def far_kernel(
    leaf_list_hbm, parent_list_ref, leaf_types_hbm, parent_types_ref, arrived_hbm, own_hbm, parents_hbm,
    m2l_hbm, l2l_hbm, l2p_hbm, near_hbm, out_ref,
    table, lists, types, tall_a, tall_b, grouped, m2l, total, flat_list, flat_types, square, narrow, l2l_ref, l2p_ref, near_ref,
    index_a, index_b, sems, in_sems,
):
    leaf_dev = out_ref.shape[0]
    boxes, entries = lists.shape
    wide = types.shape[1]
    kinds, coeffs = m2l.shape[0], m2l.shape[2]
    steps = boxes // GROUP
    loads = []
    first = 0
    for source in (arrived_hbm, own_hbm, parents_hbm):
        loads.append((source, narrow.at[pl.ds(first, source.shape[0]), :]))
        first += source.shape[0]
    loads += [(leaf_list_hbm, flat_list), (leaf_types_hbm, flat_types)]
    loads += [(l2l_hbm, l2l_ref), (l2p_hbm, l2p_ref), (near_hbm, near_ref)]
    loads = [pltpu.make_async_copy(source, target, in_sems.at[i]) for i, (source, target) in enumerate(loads)]
    for i in (3, 4, 0, 1, 2):
        loads[i].start()
    weights = pltpu.make_async_copy(m2l_hbm, m2l, sems.at[2])
    weights.start()
    for load in loads[5:]:
        load.start()
    leaf_rows = arrived_hbm.shape[0] + own_hbm.shape[0]
    tall_b[...] = jnp.zeros_like(tall_b)
    lift = 8 - lax.broadcasted_iota(I32, (1, entries), 1) % 8
    loads[3].wait()
    square[pl.ds(0, entries), :] = flat_list[...]
    lists[pl.ds(0, leaf_dev), :] = square[...].T[:, :entries] + lift
    lists[pl.ds(leaf_dev, boxes - leaf_dev), :] = parent_list_ref[...] + (lift + leaf_rows)

    def fetch(step, buffer, which):
        at = pl.multiple_of(step * GROUP, GROUP)
        return pltpu.make_async_copy(lists.at[pl.ds(at, GROUP), :], buffer, sems.at[which])

    fetch(0, index_a, 0).start()
    fetch(1, index_b, 1).start()
    types[...] = jnp.full_like(types, -1)
    loads[4].wait()
    square[pl.ds(0, entries), :] = flat_types[...]
    types[pl.ds(0, leaf_dev), pl.ds(0, entries)] = square[...].T[:, :entries]
    types[pl.ds(leaf_dev, boxes - leaf_dev), pl.ds(0, entries)] = parent_types_ref[...]
    for load in loads[:3]:
        load.wait()
    table[pl.ds(0, 8), :] = jnp.zeros((8, coeffs), F32)
    table[pl.ds(table.shape[0] - 8, 8), :] = jnp.zeros((8, coeffs), F32)
    table[pl.ds(8, narrow.shape[0]), :] = narrow[...].astype(F32)
    kinds_up = tall_a.shape[1] // QUAD
    kind_of = lax.broadcasted_iota(I32, (kinds_up, types.shape[1]), 0)
    sub = lax.broadcasted_iota(I32, (8, coeffs), 0)

    def spread(index, tall, step):
        for box in range(GROUP):
            kind = types[pl.ds(step * GROUP + box, 1), :]
            onehot = (kind_of == kind).astype(BF16)
            tiles = []
            for v in range(wide // 8):
                tile = None
                for r in range(8):
                    if v * 8 + r < entries:
                        row = table[pl.ds(index[box, v * 8 + r], 8), :]
                        tile = row if tile is None else jnp.where(sub == r, row, tile)
                tiles.append(tile)
            picked = jnp.concatenate(tiles, 0).astype(BF16)
            tall[box // QUAD, pl.ds(box % QUAD, kinds_up, stride=QUAD), :] = jnp.dot(
                onehot, picked, preferred_element_type=F32
            )

    def turn(tall, step):
        at = pl.multiple_of(step * GROUP, GROUP)
        for t in range(kinds):
            pair = [tall[h, pl.ds(t * QUAD, QUAD), :] for h in range(GROUP // QUAD)]
            grouped[t, pl.ds(at, GROUP), :] = jnp.concatenate(pair, 0).astype(BF16)

    def some(i, carry):
        for half, index, tall, done in ((0, index_a, tall_a, tall_b), (1, index_b, tall_b, tall_a)):
            step = i * 2 + half
            fetch(step, index, half).wait()
            spread(index, tall, step)
            turn(done, jnp.maximum(step - 1, 0))
            fetch(jnp.minimum(step + 2, steps - 2 + half), index, half).start()
        return carry

    lax.fori_loop(0, steps // 2, some, 0)
    for half, index in ((0, index_a), (1, index_b)):
        fetch(steps - 2 + half, index, half).wait()
    turn(tall_b, steps - 1)
    weights.wait()
    for load in loads[5:]:
        load.wait()
    total[...] = jnp.zeros_like(total)
    chunk = 52

    def multiply(first, count):
        left = jnp.concatenate([grouped[first + t] for t in range(count)], axis=1)
        right = m2l[pl.ds(first, count)].reshape(count * coeffs, coeffs)
        total[...] += jnp.dot(left, right, preferred_element_type=F32)

    def several(i, carry):
        multiply(i * chunk, chunk)
        return carry

    lax.fori_loop(0, kinds // chunk, several, 0)
    if kinds % chunk:
        multiply(kinds // chunk * chunk, kinds % chunk)
    parents = boxes - leaf_dev
    parent_local = total[pl.ds(leaf_dev, parents), :].astype(BF16)
    for octant in range(8):
        down = jnp.dot(parent_local, l2l_ref[octant], preferred_element_type=F32)
        total[pl.ds(octant, parents, stride=8), :] += down
    leaf_total = total[pl.ds(0, leaf_dev), :].astype(BF16)
    out_ref[...] = jnp.dot(leaf_total, l2p_ref[...], preferred_element_type=F32) + near_ref[...]


def far_field(leaf_list, parent_list, leaf_types, parent_types, arrived, own, parents, m2l, l2l, l2p, near):
    boxes, entries = leaf_list.shape[0] + parent_list.shape[0], leaf_list.shape[1]
    square = -(-entries // 128) * 128
    kinds, coeffs = m2l.shape[0], m2l.shape[2]
    tables = arrived.shape[0] + own.shape[0] + parents.shape[0]
    wide = -(-entries // 16) * 16
    kinds_up = -(-kinds // 16) * 16
    return pl.pallas_call(
        far_kernel,
        out_shape=jax.ShapeDtypeStruct(near.shape, F32),
        in_specs=[ANY, VMEM, ANY, VMEM] + [ANY] * 7,
        out_specs=VMEM,
        scratch_shapes=[
            pltpu.VMEM((tables + 16, coeffs), F32),
            pltpu.VMEM((boxes, entries), I32),
            pltpu.VMEM((boxes, wide), I32),
            pltpu.VMEM((GROUP // QUAD, kinds_up * QUAD, coeffs), F32),
            pltpu.VMEM((GROUP // QUAD, kinds_up * QUAD, coeffs), F32),
            pltpu.VMEM((kinds, boxes, coeffs), BF16),
            pltpu.VMEM(m2l.shape, BF16),
            pltpu.VMEM((boxes, coeffs), F32),
            pltpu.VMEM((entries, leaf_list.shape[0]), I32),
            pltpu.VMEM((entries, leaf_list.shape[0]), I32),
            pltpu.VMEM((square, leaf_list.shape[0]), I32),
            pltpu.VMEM((tables, coeffs), BF16),
            pltpu.VMEM(l2l.shape, BF16),
            pltpu.VMEM(l2p.shape, BF16),
            pltpu.VMEM(near.shape, F32),
            pltpu.SMEM((GROUP, entries), I32),
            pltpu.SMEM((GROUP, entries), I32),
            pltpu.SemaphoreType.DMA((3,)),
            pltpu.SemaphoreType.DMA((8,)),
        ],
        compiler_params=pltpu.CompilerParams(vmem_limit_bytes=58 << 20),
        name="far",
    )(leaf_list.T, parent_list, leaf_types.T, parent_types, arrived, own, parents, m2l, l2l, l2p, near)


def local(
    charges, positions, p2m, m2m, m2l, l2l, l2p,
    send_rows, send_counts, leaf_list, leaf_types, parent_list, parent_types, near_list,
):
    n_sec, n_sub = lax.axis_size("sec"), lax.axis_size("sub")
    own, arrived, parents, near = exchange(n_sec, n_sub, send_rows[0].T, charges, p2m, m2m, positions, near_list)
    parents = parents.reshape(parents.shape[0] * parents.shape[1] * parents.shape[2], parents.shape[3])
    return far_field(leaf_list, parent_list, leaf_types, parent_types, arrived, own, parents, m2l, l2l, l2p, near)


def solution(mesh):
    along = P(BOTH, None)
    in_specs = (
        along, P(None, BOTH, None), P(), P(), P(), P(), P(),
        P(BOTH, None, None), along, along, along, along, along, P(None, BOTH, None),
    )
    return jax.shard_map(local, mesh=mesh, in_specs=in_specs, out_specs=along, check_vma=False)
```
